256 devices in a mesh: lon: 32 (over y, x, core), lat: 8 (over z).
Axes of the slice: x: 4, y: 4, z: 8, core: 2. Of those that a mesh axis runs over, the one named last changes fastest.
Arguments:
- state: bfloat16 [2, 128, 4096, 256], P(None, 'lat', 'lon'), may hold values from -6 to 6
- ocean_mask: int32 [2, 128, 4096], P(None, 'lat', 'lon'), may hold values from 0 to 1, as said below
- norm_gain: float32 [256], replicated, may hold values from 0.25 to 1.75
- w_qkv: bfloat16 [256, 768], replicated
- w_out: bfloat16 [256, 256], replicated, may hold values from -0.375 to 0.375
Outputs:
- updated: bfloat16 [2, 128, 4096, 256], P(None, 'lat', 'lon')
The draws below stay inside these ranges and needn't reach their ends.
Inputs may be any that keep to these rules, and one draw needn't show every extreme that they name: `ocean_mask`: 1 marks ocean; a cell that is ocean at a level is ocean at every lower-index level.
All inputs are finite; a program needn't handle non-finite values.
Results may differ from the reference program's by a relative error of at most 0.0028.
The reference program's roundings to bfloat16 on the way count: a program that leaves them out, or rounds other values in their place, can miss the bound.
Values may be sent and summed in bfloat16 or wider, within the bound.
No kernel may reach another device: no remote copies, remote signals or barrier semaphores. Data moves between devices by JAX's collectives and lax.ppermute only.
A program may use at most 64 MiB of HBM per device.

```python
import jax
import jax.numpy as jnp
from jax import lax

C = 256
HEADS = 8
W = 16
SHIFT = 8
LEV = 2
NLAT = 128
NLON = 4096


def draw_ocean_mask(key, part):
    key = jax.random.fold_in(key, 5)
    first_key, second_key = jax.random.split(key)
    bottom_level = jax.random.randint(first_key, (NLAT, NLON), 0, LEV + 1)
    block_rows = NLAT // W
    block_cols = NLON // W
    rolled = jax.random.randint(second_key, (block_rows, block_cols), 0, 10)
    threshold = 1 + 6 * jnp.arange(block_cols, dtype=jnp.int32) // block_cols
    land_block = rolled < threshold[None, :]
    land_cells = jnp.repeat(jnp.repeat(land_block, W, axis=0), W, axis=1)
    bottom_level = jnp.where(land_cells, 0, bottom_level)
    level_index = jnp.arange(LEV, dtype=jnp.int32)[:, None, None]
    return (level_index < bottom_level[None]).astype(jnp.int32)


def draw_w_qkv(key, part):
    key = jax.random.fold_in(key, 11)
    matrix = jax.random.normal(key, (C, 3 * C), jnp.float32) * C ** (-0.5)
    return matrix.astype(jnp.bfloat16)


def shard_levels(rng, shape, cuts, smallest, largest):
    factor_of = 1.0
    for dim, blocks in cuts:
        steps = jax.random.uniform(jax.random.fold_in(jax.random.fold_in(rng, 6), dim), (blocks,), jnp.float32, smallest / len(cuts), largest / len(cuts))
        factor_of = factor_of * jnp.repeat(jnp.exp(steps), shape[dim] // blocks).reshape((-1,) + (1,) * (len(shape) - 1 - dim))
    return factor_of


def noise(key, dims, scale, limit, cuts=(), kind=jnp.bfloat16):
    gain = shard_levels(key, dims, cuts, -0.22, 0.18) if cuts else 1.0
    entries = jax.random.normal(key, dims, jnp.float32) * scale * gain
    return jnp.minimum(jnp.maximum(entries, -limit), limit).astype(kind)


def setup_inputs(seed: int = 0) -> dict:
    key_of = jax.random.split(jax.random.key(seed), 6)
    state = noise(key_of[0], (LEV, NLAT, NLON, C), 1.0, 6.0, ((1, 8), (2, 32)))
    ocean_mask = draw_ocean_mask(jax.random.fold_in(key_of[5], 71), 0)
    norm_gain = jnp.clip(1.0 + 0.15 * jax.random.normal(key_of[2], (C,), jnp.float32), 0.25, 1.75)
    w_qkv = draw_w_qkv(jax.random.fold_in(key_of[5], 71), 0)
    w_out = noise(key_of[4], (C, C), C ** -0.5, 0.375)
    return {"state": state, "ocean_mask": ocean_mask, "norm_gain": norm_gain, "w_qkv": w_qkv, "w_out": w_out}


def window_update(tokens, ocean, norm_gain, w_qkv, w_out):
    values_f = tokens.astype(jnp.float32)
    average = lax.optimization_barrier(jnp.mean(values_f, axis=1, keepdims=True))
    spread_sq = lax.optimization_barrier(jnp.mean((values_f - average) ** 2, axis=1, keepdims=True))
    normed = ((values_f - average) * lax.rsqrt(spread_sq + 1e-05) * norm_gain).astype(jnp.bfloat16)
    projected = jnp.dot(normed, w_qkv, preferred_element_type=jnp.float32)
    head_size = C // HEADS
    queries = (projected[:, :C] * (1.0 / head_size ** 0.5)).astype(jnp.bfloat16)
    keys_bf = projected[:, C:2 * C].astype(jnp.bfloat16)
    values_bf = projected[:, 2 * C:].astype(jnp.bfloat16)
    count = tokens.shape[0]
    queries = queries.reshape(count, HEADS, head_size).transpose(1, 0, 2)
    keys_bf = keys_bf.reshape(count, HEADS, head_size).transpose(1, 0, 2)
    values_bf = values_bf.reshape(count, HEADS, head_size).transpose(1, 0, 2)
    allowed = ocean[None, :] > 0

    def one_head(pieces):
        query_h, key_h, value_h = pieces
        scores = jnp.dot(query_h, key_h.T, preferred_element_type=jnp.float32)
        top_score = lax.optimization_barrier(jnp.max(jnp.where(allowed, scores, -1e+30), axis=1, keepdims=True))
        weights = jnp.where(allowed, jnp.exp(jnp.where(allowed, scores - top_score, 0.0)), 0.0)
        total = lax.optimization_barrier(jnp.sum(weights, axis=1)) + (1.0 - ocean)
        mixed = jnp.dot(weights.astype(jnp.bfloat16), value_h, preferred_element_type=jnp.float32)
        return mixed / total[:, None]
    mixed = lax.map(one_head, (queries, keys_bf, values_bf))
    mixed = mixed.transpose(1, 0, 2).reshape(count, C).astype(jnp.bfloat16)
    delta = jnp.dot(mixed, w_out, preferred_element_type=jnp.float32) * ocean[:, None]
    return delta.astype(jnp.bfloat16)

def to_windows(grid):
    rest = grid.shape[3:]
    levels_n, rows_n, cols_n = (grid.shape[0], grid.shape[1], grid.shape[2])
    shaped = grid.reshape((levels_n, rows_n // W, W, cols_n // W, W) + rest)
    order = (1, 3, 2, 4, 0) + tuple(range(5, 5 + len(rest)))
    return shaped.transpose(order).reshape((rows_n // W * (cols_n // W), W * W * levels_n) + rest)

def from_windows(blocks, levels_n, rows_n, cols_n):
    width = blocks.shape[-1]
    shaped = blocks.reshape(rows_n // W, cols_n // W, W, W, levels_n, width)
    return shaped.transpose(4, 0, 2, 1, 3, 5).reshape(levels_n, rows_n, cols_n, width)

def reference(state, ocean_mask, norm_gain, w_qkv, w_out):
    ocean_f = ocean_mask.astype(jnp.float32)
    ghost_state = state[:, NLAT - SHIFT:][:, ::-1, ::-1]
    ghost_mask = ocean_f[:, NLAT - SHIFT:][:, ::-1, ::-1]
    extended = jnp.concatenate([state, ghost_state], axis=1)
    extended_mask = jnp.concatenate([ocean_f, ghost_mask], axis=1)
    shifted = jnp.roll(extended[:, SHIFT:], -SHIFT, axis=2)
    shifted_mask = jnp.roll(extended_mask[:, SHIFT:], -SHIFT, axis=2)
    win_state = to_windows(shifted)
    win_mask = to_windows(shifted_mask)

    def per_window(pieces):
        return window_update(pieces[0], pieces[1], norm_gain, w_qkv, w_out)
    deltas = lax.map(per_window, (win_state, win_mask))
    delta = from_windows(deltas, LEV, NLAT, NLON)
    rolled = jnp.roll(delta, SHIFT, axis=2)
    placed = jnp.concatenate([jnp.zeros((LEV, SHIFT, NLON, C), jnp.bfloat16), rolled[:, :NLAT - SHIFT]], axis=1)
    return (state.astype(jnp.float32) + placed.astype(jnp.float32)).astype(jnp.bfloat16)
```

```python
import functools

import jax
import jax.numpy as jnp
from jax import lax
from jax.experimental import pallas as pl
from jax.experimental.pallas import tpu as pltpu
from jax.sharding import PartitionSpec as P

C = 256
HEADS = 8
HEAD = C // HEADS
W = 16
SHIFT = 8
LEV = 2
HALF = W * W * LEV // 2
TOK = 2 * HALF
BLK = HALF // 2
QB = 32
LAND = 1024.0
SIZES = (128, 256, 304, 512)


def dot_nt(a, b):
    return lax.dot_general(a, b, (((1,), (1,)), ((), ())), preferred_element_type=jnp.float32)


def dot_nn(a, b):
    return jnp.dot(a, b, preferred_element_type=jnp.float32)


def attend(own, count, q_from, q_to, row_rank, size, gain_ref, wq_ref, wk_ref, wvt_ref, hm_ref, tok_ref, q_ref, k_ref, vt_ref, mix_ref):
    slot = lax.broadcasted_iota(jnp.int32, (size, 1), 0) + 1
    wanted = jnp.minimum(slot, count).astype(jnp.float32)
    pick = jnp.where(row_rank == wanted, 1.0, 0.0).astype(jnp.bfloat16)
    tokens = dot_nn(pick, tok_ref[...])
    average = jnp.mean(tokens, axis=1, keepdims=True)
    centred = tokens - average
    spread_sq = jnp.mean(centred * centred, axis=1, keepdims=True)
    normed = (centred * lax.rsqrt(spread_sq + 1e-05) * gain_ref[...]).astype(jnp.bfloat16)
    q_rows = min(size, HALF)
    q_ref[:q_rows, :] = (dot_nn(normed[:q_rows], wq_ref[...]) * (1.0 / HEAD**0.5)).astype(jnp.bfloat16)
    k_ref[:size, :] = dot_nn(normed, wk_ref[...]).astype(jnp.bfloat16)
    valid = lax.broadcasted_iota(jnp.int32, (1, size), 1) < count
    vt_ref[:C, :size] = jnp.where(valid, dot_nt(wvt_ref[...], normed), 0.0).astype(jnp.bfloat16)
    vt_ref[C:, :size] = jnp.where(jnp.broadcast_to(valid, (W, size)), 1.0, 0.0).astype(jnp.bfloat16)

    def block(b, carry):
        at = pl.multiple_of(b * QB, QB)
        queries = q_ref[pl.ds(at, QB), :]
        stacked = jnp.concatenate([queries] * HEADS, axis=0) * hm_ref[...]
        scores = dot_nt(k_ref[:size, :], stacked)
        top = jnp.max(scores, axis=0, keepdims=True)
        weights = jnp.exp(scores - top).astype(jnp.bfloat16)
        summed = dot_nn(vt_ref[:, :size], weights)
        slot_q = at + lax.broadcasted_iota(jnp.int32, (1, C), 1) % QB
        total = summed[C : C + 1, :] + jnp.where(slot_q < own, 0.0, 1.0)
        mixed = (summed[:C, :] * (1.0 / total)).astype(jnp.bfloat16) * hm_ref[...]
        fold = jnp.where(
            lax.broadcasted_iota(jnp.int32, (QB, C), 1) % QB == lax.broadcasted_iota(jnp.int32, (QB, C), 0), 1.0, 0.0
        ).astype(jnp.bfloat16)
        mix_ref[pl.ds(at, QB), :] = dot_nt(fold, mixed).astype(jnp.bfloat16)
        return carry

    lax.fori_loop(q_from // QB, (q_to + QB - 1) // QB, block, 0)


def windows_kernel(edges, flags, own0, own1, below, above, folded, gain, wq, wk, wvt, wout, hm, tri, eye, out, tok, q_s, k_s, vt_s, mix_s):
    k = pl.program_id(0)
    r = pl.program_id(1)
    last = pl.num_programs(0) - 1

    @pl.when((k == 0) & (r == 0))
    def _():
        mix_s[...] = jnp.zeros_like(mix_s)

    @pl.when(r == 0)
    def _():
        tok[:HALF, :] = own0[...].reshape(HALF, C)
        tok[HALF:, :] = below[...].reshape(HALF, C)

    @pl.when(r == 1)
    def _():
        tok[:HALF, :] = own1[...].reshape(HALF, C)

    @pl.when((r == 1) & (flags[1] == 1))
    def _():
        tok[HALF:, :] = folded[...].reshape(HALF, C)

    @pl.when((r == 1) & (flags[1] == 0))
    def _():
        tok[HALF:, :] = above[...].reshape(HALF, C)

    first = jnp.where(lax.broadcasted_iota(jnp.int32, (16, C), 1) == 0, 1.0, 0.0).astype(jnp.bfloat16)
    ocean = dot_nt(first, tok[...]) < LAND / 2
    ocean_f = jnp.where(ocean, 1.0, 0.0)
    rank = dot_nn(ocean_f.astype(jnp.bfloat16), tri[...]) * ocean_f
    row_rank = rank[0:1, :]
    count_a = jnp.max(row_rank[:, :BLK]).astype(jnp.int32)
    own = jnp.maximum(count_a, jnp.max(row_rank[:, BLK:HALF]).astype(jnp.int32))
    count = jnp.maximum(own, jnp.max(row_rank[:, HALF:]).astype(jnp.int32))
    q_from, q_to = 0, own
    if edges:
        q_from = jnp.where(k == 0, count_a, 0)
        q_to = jnp.where(k == last, count_a, own)
    active = (q_to > q_from) & ((r == 1) | (flags[0] == 0))

    @pl.when(jnp.logical_not(active))
    def _():
        out[...] = jnp.zeros_like(out)

    below_size = 0
    for size in SIZES:

        @pl.when(active & (count > below_size) & (count <= size))
        def _(size=size):
            attend(own, count, q_from, q_to, row_rank, size, gain, wq, wk, wvt, hm, tok, q_s, k_s, vt_s, mix_s)

        below_size = size

    @pl.when(active)
    def _():
        delta = dot_nn(mix_s[...], wout[...]).astype(jnp.bfloat16)
        ranks = jnp.broadcast_to(row_rank[:, :HALF], (HALF, HALF)).astype(jnp.bfloat16)
        col_rank = dot_nt(eye[...], ranks)
        spread = jnp.where(
            col_rank == (lax.broadcasted_iota(jnp.int32, (HALF, HALF), 1) + 1).astype(jnp.float32), 1.0, 0.0
        ).astype(jnp.bfloat16)
        out[...] = dot_nn(spread, delta).astype(jnp.bfloat16).reshape(out.shape)


def window_deltas(edges, flags, own0, own1, below, above, folded, consts):
    n = own0.shape[0] // 2
    pair = lambda k, r, flags: (k, 0, 0)
    mirror = lambda k, r, flags: (n - 1 - k, 0, 0)
    halves = pl.BlockSpec((2, BLK, C), pair)
    whole = [pl.BlockSpec(c.shape, lambda k, r, flags: (0, 0)) for c in consts]
    return pl.pallas_call(
        functools.partial(windows_kernel, edges),
        out_shape=jax.ShapeDtypeStruct((n, 2, 2, BLK, C), jnp.bfloat16),
        grid_spec=pltpu.PrefetchScalarGridSpec(
            num_scalar_prefetch=1,
            grid=(n, 2),
            in_specs=[halves] * 4 + [pl.BlockSpec((2, BLK, C), mirror)] + whole,
            out_specs=pl.BlockSpec((1, 1, 2, BLK, C), lambda k, r, flags: (k, r, 0, 0, 0)),
            scratch_shapes=[
                pltpu.VMEM((TOK, C), jnp.bfloat16),
                pltpu.VMEM((HALF, C), jnp.bfloat16),
                pltpu.VMEM((TOK, C), jnp.bfloat16),
                pltpu.VMEM((C + W, TOK), jnp.bfloat16),
                pltpu.VMEM((HALF, C), jnp.bfloat16),
            ],
        ),
        compiler_params=pltpu.CompilerParams(vmem_limit_bytes=40 * 1024 * 1024),
        cost_estimate=pl.CostEstimate(flops=n * 10**9, bytes_accessed=n * 10**6, transcendentals=0),
        name="windows_edge" if edges else "windows_inner",
    )(flags, own0, own1, below, above, folded, *consts)


def permute(x, pairs):
    return lax.ppermute(x, ("lon", "lat"), pairs)


def shards(state, ocean_mask, norm_gain, w_qkv, w_out):
    lon_n, lat_n = lax.axis_size("lon"), lax.axis_size("lat")
    lat = lax.axis_index("lat")
    at = lambda i, j: i * lat_n + j
    every = [(i, j) for i in range(lon_n) for j in range(lat_n)]
    go_down = [(at(i, j), at(i, j - 1)) for i, j in every if j > 0]
    go_up = [(at(i, j), at(i, j + 1)) for i, j in every if j < lat_n - 1]
    go_fold = [(at(i, lat_n - 1), at(lon_n - 1 - i, lat_n - 1)) for i in range(lon_n)]
    go_east = [(at(i, j), at((i + 1) % lon_n, j)) for i, j in every]
    go_west = [(at(i, j), at((i - 1) % lon_n, j)) for i, j in every]

    rows, cols = state.shape[1], state.shape[2]
    n_blk = cols // SHIFT
    marked = jnp.where(ocean_mask[..., None] > 0, state, jnp.bfloat16(LAND))
    parts = marked.reshape(LEV, 2, SHIFT, n_blk, SHIFT, C).transpose(1, 3, 0, 2, 4, 5).reshape(2, n_blk, BLK, C)

    down_1, up_1 = parts[0, 3:13], parts[1, 3:13]
    below_1 = permute(up_1, go_up)
    above_1 = permute(down_1, go_down)
    from_west = permute(parts[:, n_blk - 1], go_east)
    from_east = permute(parts[:, 0], go_west)
    fold_1 = permute(up_1, go_fold)
    down_2 = jnp.concatenate([from_west[0:1], parts[0, 0:3], parts[0, 13:16], from_east[0:1]])
    up_2 = jnp.concatenate([from_west[1:2], parts[1, 0:3], parts[1, 13:16], from_east[1:2]])
    below_2 = permute(up_2, go_up)
    above_2 = permute(down_2, go_down)
    fold_2 = permute(up_2, go_fold)

    row = lax.broadcasted_iota(jnp.int32, (TOK, TOK), 0)
    col = lax.broadcasted_iota(jnp.int32, (TOK, TOK), 1)
    one = lambda cond: jnp.where(cond, 1.0, 0.0).astype(jnp.bfloat16)
    head_mask = one(row[:C, :C] // HEAD == col[:C, :C] // HEAD)
    consts = (
        norm_gain[None, :],
        w_qkv[:, :C],
        w_qkv[:, C : 2 * C],
        w_qkv[:, 2 * C :].T,
        w_out,
        head_mask,
        one(row <= col),
        one(row[:HALF, :HALF] == col[:HALF, :HALF]),
    )
    flags = jnp.stack([lat == 0, lat == lat_n - 1]).astype(jnp.int32)
    delta_1 = window_deltas(False, flags, down_1, up_1, below_1, above_1, fold_1, consts)
    delta_2 = window_deltas(True, flags, down_2, up_2, below_2, above_2, fold_2, consts)
    inner = delta_1.transpose(1, 0, 2, 3, 4).reshape(2, 10, BLK, C)
    outer = delta_2.transpose(1, 0, 2, 3, 4).reshape(2, 8, BLK, C)
    delta = jnp.concatenate([outer[:, 1:4], inner, outer[:, 4:7]], axis=1)
    delta = delta.reshape(2, n_blk, LEV, SHIFT, SHIFT, C).transpose(2, 0, 3, 1, 4, 5).reshape(LEV, rows, cols, C)
    return (state.astype(jnp.float32) + delta.astype(jnp.float32)).astype(jnp.bfloat16)


def solution(mesh):
    in_specs = (P(None, "lat", "lon", None), P(None, "lat", "lon"), P(), P(), P())
    out_specs = P(None, "lat", "lon", None)
    return jax.shard_map(shards, mesh=mesh, in_specs=in_specs, out_specs=out_specs, check_vma=False)
```

```python
import functools

import jax
import jax.numpy as jnp
from jax import lax
from jax.experimental import pallas as pl
from jax.experimental.pallas import tpu as pltpu
from jax.sharding import PartitionSpec as P

C = 256
HEADS = 8
HEAD = C // HEADS
W = 16
SHIFT = 8
LEV = 2
HALF = W * W * LEV // 2
BLK = HALF // 2
QB = 32
ONES = 16
SMALL = 160
LAND = 1024.0
SAFE_SQ = 60.0**2

VMEM = pl.BlockSpec(memory_space=pltpu.VMEM)
SMEM = pl.BlockSpec(memory_space=pltpu.SMEM)
ANY = pl.BlockSpec(memory_space=pl.ANY)
PARAMS = pltpu.CompilerParams(vmem_limit_bytes=36 * 1024 * 1024)


def dot_nt(a, b):
    return lax.dot_general(a, b, (((1,), (1,)), ((), ())), preferred_element_type=jnp.float32)


def dot_nn(a, b):
    return jnp.dot(a, b, preferred_element_type=jnp.float32)


def iota(shape, axis):
    return lax.broadcasted_iota(jnp.int32, shape, axis)


def one(condition):
    return jnp.where(condition, 1.0, 0.0).astype(jnp.bfloat16)


def ocean_ranks(halves, rows_n):
    channel, row = iota((rows_n, C), 1), iota((rows_n, C), 0)
    marks = None
    for i, half in enumerate(halves):
        part = dot_nt(one((channel == 0) & (row == i)), half)
        marks = part if marks is None else marks + part
    ocean = jnp.where(marks < LAND / 2, 1.0, 0.0)
    return dot_nn(ocean.astype(jnp.bfloat16), one(iota((C, C), 0) <= iota((C, C), 1))) * ocean


def packed_norm(tokens, ranks, count, size, gain):
    wanted = jnp.minimum(iota((size, 1), 0) + 1, count).astype(jnp.float32)
    packed = dot_nn(one(ranks == wanted), tokens)
    average = jnp.mean(packed, axis=1, keepdims=True)
    centred = packed - average
    spread_sq = jnp.mean(centred * centred, axis=1, keepdims=True)
    return (centred * lax.rsqrt(spread_sq + 1e-05) * gain).astype(jnp.bfloat16)


def valid_values(values, count, size):
    valid = iota((1, size), 1) < count
    return jnp.where(valid, values, 0.0).astype(jnp.bfloat16), one(jnp.broadcast_to(valid, (ONES, size)))


def head_norms(keys, sums):
    return jnp.max(dot_nn((keys * keys).astype(jnp.bfloat16), sums), axis=0, keepdims=True)


def fill(keys, values, i, key, size):
    keys[i, size:, :] = jnp.broadcast_to(key[0:1].astype(jnp.float32), (HALF - size, C)).astype(jnp.bfloat16)
    values[i, :, size:] = jnp.zeros((C + ONES, HALF - size), jnp.bfloat16)


def prep_kernel(flags, state, mask, part_a, part_b, held, sems):
    blocks = part_a.shape[0]
    cols = blocks * SHIFT
    half = SHIFT // 2
    chunks = [(s, level, g) for s in range(2) for level in range(LEV) for g in range(2)]
    copies = []
    for i, (s, level, g) in enumerate(chunks):
        start = jnp.where(flags[2] == s, SHIFT, 0) + half * g
        copies.append(pltpu.make_async_copy(state.at[level, pl.ds(start, half)], held.at[i], sems.at[i]))
        copies[-1].start()
    eye = one(iota((cols, cols), 0) == iota((cols, cols), 1))
    by_column = [dot_nt(eye, mask[level].astype(jnp.float32).astype(jnp.bfloat16)) for level in range(LEV)]
    for i, (s, level, g) in enumerate(chunks):
        part = (part_a, part_b)[s]
        upper = flags[2] == s
        copies[i].wait()
        for p in range(half // 2):
            pair = []
            for row in (2 * p, 2 * p + 1):
                at = half * g + row
                ocean = jnp.where(upper, by_column[level][:, SHIFT + at : SHIFT + at + 1], by_column[level][:, at : at + 1])
                pair.append(jnp.where(ocean > 0.5, held[i, row].astype(jnp.float32), LAND).reshape(blocks, SHIFT, C))
            at = (BLK // 2) * level + SHIFT * (half * g + 2 * p)
            part[:, at : at + 2 * SHIFT, :] = jnp.concatenate(pair, axis=1).astype(jnp.bfloat16)


def prep(flags, state, mask):
    blocks = state.shape[2] // SHIFT
    shape = jax.ShapeDtypeStruct((blocks, BLK, C), jnp.bfloat16)
    return pl.pallas_call(
        prep_kernel,
        out_shape=(shape, shape),
        in_specs=[SMEM, ANY, VMEM],
        out_specs=(VMEM, VMEM),
        scratch_shapes=[
            pltpu.VMEM((2 * LEV * 2, SHIFT // 2, state.shape[2], C), jnp.bfloat16),
            pltpu.SemaphoreType.DMA((2 * LEV * 2,)),
        ],
        compiler_params=pltpu.CompilerParams(vmem_limit_bytes=58 * 1024 * 1024),
        name="windows_prep",
    )(flags, state, mask)


def edge_parts(flags, state, mask, start):
    cut = jnp.where(mask[:, :, start : start + SHIFT, None] > 0, state[:, :, start : start + SHIFT], jnp.bfloat16(LAND))
    lower, upper = [cut[:, SHIFT * r : SHIFT * r + SHIFT].reshape(BLK, C) for r in range(2)]
    odd = flags[2] == 1
    return jnp.stack([jnp.where(odd, lower, upper), jnp.where(odd, upper, lower)])


def finish_kernel(flags, state, inner, outer, out):
    level, r = pl.program_id(0), pl.program_id(1)
    s = jnp.where(r == 1, flags[2], 1 - flags[2])
    blocks = state.shape[2] // SHIFT
    for p in range(SHIFT // 2):
        at = pl.multiple_of(level * (BLK // 2) + 2 * SHIFT * p, 2 * SHIFT)
        deltas = []
        for b in range(blocks):
            if b == 0 or b == blocks - 1:
                delta = outer[b // (blocks - 1), s, 0, pl.ds(at, 2 * SHIFT), :]
            else:
                delta = inner[(b - 1) // 2, s, (b - 1) % 2, pl.ds(at, 2 * SHIFT), :]
            deltas.append(delta.astype(jnp.float32))
        for i in range(2):
            added = jnp.concatenate([d[SHIFT * i : SHIFT * i + SHIFT] for d in deltas], axis=0)
            out[0, 2 * p + i] = (state[0, 2 * p + i].astype(jnp.float32) + added).astype(jnp.bfloat16)


def finish(flags, state, inner, outer):
    levels, rows, cols, _ = state.shape
    block = pl.BlockSpec((1, SHIFT, cols, C), lambda l, r, flags: (l, r, 0, 0))
    whole = lambda x: pl.BlockSpec(x.shape, lambda l, r, flags: (0,) * x.ndim)
    return pl.pallas_call(
        finish_kernel,
        out_shape=jax.ShapeDtypeStruct(state.shape, state.dtype),
        grid_spec=pltpu.PrefetchScalarGridSpec(
            num_scalar_prefetch=1,
            grid=(levels, 2),
            in_specs=[block, pl.BlockSpec(memory_space=pltpu.VMEM), pl.BlockSpec(memory_space=pltpu.VMEM)],
            out_specs=block,
        ),
        compiler_params=PARAMS,
        name="windows_finish",
    )(flags, state, inner, outer)


def near_kernel(edges, n, part_a, part_b, west, east, gain, w_qkv, k_out, vt_out, qt_out, spread_out, counts, peaks, edge, ranks, wqt, wvt, norms):
    parts = (part_a, part_b)
    last = part_a.shape[0] - 1
    if edges:
        for s in range(2):
            edge[s, 0], edge[s, 1] = parts[s][0], west[s]
            edge[s, 2], edge[s, 3] = parts[s][last], east[s]

    def tokens_at(w, s):
        if edges:
            return edge[s, pl.ds(2 * w, 2)].reshape(HALF, C)
        return parts[s][pl.ds(2 * w + 1, 2)].reshape(HALF, C)

    rank = ocean_ranks([tokens_at(i // 2, i % 2) for i in range(2 * n)], 16)
    ranks[...] = rank
    for i in range(2 * n):
        counts[i] = jnp.max(rank[i : i + 1, :]).astype(jnp.int32)
        counts[2 * n + i] = jnp.max(rank[i : i + 1, :BLK]).astype(jnp.int32) if edges else counts[i]

    eye = one(iota((C, C), 0) == iota((C, C), 1))
    wqt[...] = dot_nt(eye, w_qkv[:, :C]).astype(jnp.bfloat16)
    wvt[...] = dot_nt(eye, w_qkv[:, 2 * C :]).astype(jnp.bfloat16)
    norms[...] = jnp.zeros_like(norms)
    by_column = dot_nt(eye, rank.astype(jnp.bfloat16))
    for i in range(2 * n):
        col_rank = jnp.broadcast_to(by_column[:, i : i + 1], (HALF, BLK))
        for at in (0, BLK):
            number = (iota((HALF, BLK), 1) + (at + 1)).astype(jnp.float32)
            spread_out[i, :, at : at + BLK] = one(col_rank == number)

    def window(size, w):
        sums = one(iota((C, BLK), 0) // HEAD == iota((C, BLK), 1))
        sums_t = one(iota((ONES, C), 1) // HEAD == iota((ONES, C), 0))
        count = [counts[2 * w + s] for s in range(2)]
        normed = [
            packed_norm(tokens_at(w, s), ranks[pl.ds(2 * w + s, 1), :], count[s], size, gain[...]) for s in range(2)
        ]
        keys = [dot_nn(x, w_qkv[:, C : 2 * C]).astype(jnp.bfloat16) for x in normed]
        queries = [(dot_nt(wqt[...], x) * (1.0 / HEAD**0.5)).astype(jnp.bfloat16) for x in normed]
        values = [valid_values(dot_nt(wvt[...], x), c, size) for x, c in zip(normed, count)]
        for s in range(2):
            k_out[2 * w + s, :size, :] = keys[s]
            qt_out[2 * w + s, :, :size] = queries[s]
            vt_out[2 * w + s, :C, :size] = values[s][0]
            vt_out[2 * w + s, C:, :size] = values[s][1]
            if size < HALF:
                qt_out[2 * w + s, :, size:] = jnp.zeros((C, HALF - size), jnp.bfloat16)
                fill(k_out, vt_out, 2 * w + s, keys[s], size)
            norms[0:1, :] = jnp.maximum(norms[0:1, :], head_norms(keys[s], sums))
            by_head = dot_nn(sums_t, queries[s] * queries[s])
            norms[8:, :] = jnp.maximum(norms[8:, :], jnp.max(by_head, axis=1, keepdims=True))

    def either(w, carry):
        largest = jnp.maximum(counts[2 * w], counts[2 * w + 1])
        for size, fits in ((SMALL, largest <= SMALL), (HALF, largest > SMALL)):
            pl.when(fits)(functools.partial(window, size, w))
        return carry

    lax.fori_loop(0, n, either, 0)
    peaks[0] = jnp.max(norms[0:1, :])
    peaks[1] = jnp.max(norms[8:, :])


def near_half(edges, part_a, part_b, west, east, gain, w_qkv):
    n = 2 if edges else part_a.shape[0] // 2 - 1
    bf = lambda *shape: jax.ShapeDtypeStruct(shape, jnp.bfloat16)
    return pl.pallas_call(
        functools.partial(near_kernel, edges, n),
        out_shape=(
            bf(2 * n, HALF, C),
            bf(2 * n, C + ONES, HALF),
            bf(2 * n, C, HALF),
            bf(2 * n, HALF, HALF),
            jax.ShapeDtypeStruct((4 * n,), jnp.int32),
            jax.ShapeDtypeStruct((2,), jnp.float32),
        ),
        in_specs=[VMEM] * 6,
        out_specs=(VMEM,) * 4 + (SMEM,) * 2,
        scratch_shapes=[
            pltpu.VMEM((2, 4, BLK, C), jnp.bfloat16),
            pltpu.VMEM((16, C), jnp.float32),
            pltpu.VMEM((C, C), jnp.bfloat16),
            pltpu.VMEM((C, C), jnp.bfloat16),
            pltpu.VMEM((8 + ONES, BLK), jnp.float32),
        ],
        compiler_params=PARAMS,
        cost_estimate=pl.CostEstimate(flops=n * 10**9, bytes_accessed=n * 10**6, transcendentals=0),
        name="windows_near_edge" if edges else "windows_near",
    )(part_a, part_b, west, east, gain, w_qkv)


def tops(scores, bounded):
    if bounded:
        return scores
    top = jnp.maximum(jnp.max(scores[0], axis=0, keepdims=True), jnp.max(scores[1], axis=0, keepdims=True))
    return [score - top for score in scores]


def mix(scores, values, slots, queries_n):
    parts = [dot_nn(value, jnp.exp(score).astype(jnp.bfloat16)) for score, value in zip(scores, values)]
    summed = parts[0] + parts[1]
    n = summed.shape[0] - ONES
    total = summed[n : n + 1, :] + jnp.where(slots < queries_n, 0.0, 1.0)
    return summed[:n, :] * (1.0 / total)


def far_kernel(
    edges, n, flags, counts, peaks, far_a, far_b, corner_a, corner_b, gain, w_qkv, w_out, k_near, vt_near, qt, spread, out,
    edge, ranks, k_far, vt_far, wvt, woutt, norms, rem, mixes, count_far,
):
    far_refs, corners = (far_a, far_b), (corner_a, corner_b)
    last = far_a.shape[0] - 1
    top = flags[1]
    if edges:
        for s in range(2):
            for e in range(2):
                i = jnp.where(top == 1, 1 - e, e) if s == 1 else e
                edge[s, 2 * e] = far_refs[s][last * i]
                edge[s, 2 * e + 1] = corners[s][i]

    def tokens_at(w, s):
        if edges:
            return edge[s, pl.ds(2 * w, 2)].reshape(HALF, C)
        i = jnp.where(top == 1, n - 1 - w, w) if s == 1 else w
        return far_refs[s][pl.ds(2 * i + 1, 2)].reshape(HALF, C)

    rank = ocean_ranks([tokens_at(i // 2, i % 2) for i in range(2 * n)], 16)
    ranks[...] = rank
    for i in range(2 * n):
        found = jnp.max(rank[i : i + 1, :]).astype(jnp.int32)
        count_far[i] = jnp.where(flags[0] == 1, 0, found) if i % 2 else found
    eye = one(iota((C, C), 0) == iota((C, C), 1))
    wvt[...] = dot_nt(eye, w_qkv[:, 2 * C :]).astype(jnp.bfloat16)
    woutt[...] = dot_nt(eye, w_out[...]).astype(jnp.bfloat16)
    norms[...] = jnp.zeros_like(norms)

    def both(j):
        windows = (2 * j, jnp.minimum(2 * j + 1, n - 1))
        return [(w, s) for w in windows for s in range(2)]

    def prepare(size, j):
        sums = one(iota((C, BLK), 0) // HEAD == iota((C, BLK), 1))
        items = both(j)
        count = [count_far[2 * w + s] for w, s in items]
        normed = [
            packed_norm(tokens_at(w, s), ranks[pl.ds(2 * w + s, 1), :], c, size, gain[...]) for (w, s), c in zip(items, count)
        ]
        keys = [dot_nn(x, w_qkv[:, C : 2 * C]) for x in normed]
        values = [valid_values(dot_nt(wvt[...], x), c, size) for x, c in zip(normed, count)]
        for (w, s), c, key, value in zip(items, count, keys, values):
            spare = jnp.broadcast_to(k_near[2 * w + s, 0:1, :].astype(jnp.float32), (size, C))
            key = jnp.where(c > 0, key, spare).astype(jnp.bfloat16)
            k_far[2 * w + s, :size, :] = key
            vt_far[2 * w + s, :C, :size] = value[0]
            vt_far[2 * w + s, C:, :size] = value[1]
            if size < HALF:
                fill(k_far, vt_far, 2 * w + s, key, size)
            norms[0:1, :] = jnp.maximum(norms[0:1, :], head_norms(key, sums))

    def ready(j, carry):
        largest = functools.reduce(jnp.maximum, [count_far[2 * w + s] for w, s in both(j)])
        for size, fits in ((SMALL, largest <= SMALL), (HALF, largest > SMALL)):
            pl.when(fits)(functools.partial(prepare, size, j))
        return carry

    lax.fori_loop(0, (n + 1) // 2, ready, 0)
    peak = jnp.maximum(jnp.max(norms[0:1, :]), peaks[0]) * peaks[1]
    safe = peak <= SAFE_SQ

    lane = iota((1, C), 1)

    def attend(w, halves, size, bounded):
        asked = {s: counts[2 * n + 2 * w + s] for s in halves}
        at = {s: 2 * w + s for s in halves}
        keys = {s: [k_near[at[s], :size, :], k_far[2 * w + s, :size, :]] for s in halves}

        def values(s, rows):
            return [
                jnp.concatenate([ref[i, rows, :size], ref[i, C : C + ONES, :size]], axis=0)
                for ref, i in ((vt_near, at[s]), (vt_far, 2 * w + s))
            ]

        def tile_scores(t, s):
            g = t // 2
            none = jnp.zeros((HEAD, BLK), jnp.bfloat16)
            rows = []
            for h in range(4 * g, 4 * g + 4):
                mine = qt[at[s], HEAD * h : HEAD * h + HEAD, :BLK] if h // 2 == t else none
                rows.append(jnp.concatenate([mine, none] if h % 2 == 0 else [none, mine], axis=1))
            stacked = jnp.concatenate(rows, axis=0)
            return [dot_nn(key[:, BLK * g : BLK * g + BLK], stacked) for key in keys[s]]

        tiles = [(t, s) for t in range(4) for s in halves]
        ahead = tile_scores(*tiles[0])
        for i, (t, s) in enumerate(tiles):
            now = ahead
            if i + 1 < len(tiles):
                ahead = tile_scores(*tiles[i + 1])
            mixed = mix(tops(now, bounded), values(s, slice(64 * t, 64 * t + 64)), lane % BLK, asked[s])
            mixes[2 * w + s, 64 * t : 64 * t + HEAD, :BLK] = mixed[:HEAD, :BLK].astype(jnp.bfloat16)
            mixes[2 * w + s, 64 * t + HEAD : 64 * t + 64, :BLK] = mixed[HEAD:, BLK:].astype(jnp.bfloat16)

        most = functools.reduce(jnp.maximum, asked.values())
        for s in halves:
            rem[s] = jnp.zeros_like(rem[s])

        def more(b, carry):
            start = b * QB
            sub, lan = iota((C, C), 0), iota((C, C), 1)
            block = sub // HEAD == lan // QB
            repeat = one(sub[:BLK] + BLK == start + lan[:BLK] % QB)
            place = one(sub[:, :BLK] % QB + start == lan[:, :BLK] + BLK)
            stacked = [jnp.where(block, dot_nn(qt[at[s], :, BLK:], repeat), 0.0).astype(jnp.bfloat16) for s in halves]
            scores = [[dot_nn(key, x) for key in keys[s]] for s, x in zip(halves, stacked)]
            mixed = [
                mix(tops(score, bounded), values(s, slice(0, C)), start + lane % QB, asked[s]) for s, score in zip(halves, scores)
            ]
            mixed = [jnp.where(block, x, 0.0).astype(jnp.bfloat16) for x in mixed]
            placed = [dot_nn(x, place) for x in mixed]
            for s, x in zip(halves, placed):
                rem[s] = (rem[s].astype(jnp.float32) + x).astype(jnp.bfloat16)
            return carry

        lax.fori_loop(BLK // QB, (most + QB - 1) // QB, more, 0)
        for s in halves:
            mixes[2 * w + s, :, BLK:] = rem[s]

    def window(w, carry):
        at = 2 * w
        largest = jnp.maximum(jnp.maximum(counts[at], counts[at + 1]), jnp.maximum(count_far[2 * w], count_far[2 * w + 1]))
        active = jnp.maximum(counts[2 * n + at], counts[2 * n + at + 1]) > 0

        @pl.when(jnp.logical_not(active))
        def _():
            for s in range(2):
                mixes[2 * w + s] = jnp.zeros_like(mixes[2 * w + s])

        pl.when(active & safe & (largest <= SMALL))(functools.partial(attend, w, (0, 1), SMALL, True))
        pl.when(active & safe & (largest > SMALL))(functools.partial(attend, w, (0, 1), HALF, True))
        for s in range(2):
            pl.when(active & jnp.logical_not(safe))(functools.partial(attend, w, (s,), HALF, False))
        return carry

    lax.fori_loop(0, n, window, 0)

    def project(j, carry):
        items = both(j)
        delta_t = [dot_nn(woutt[...], mixes[2 * w + s]).astype(jnp.bfloat16) for w, s in items]
        delta = [dot_nt(spread[2 * w + s], x) for (w, s), x in zip(items, delta_t)]
        for (w, s), x in zip(items, delta):
            if s == 1:
                x = jnp.where(flags[0] == 1, 0.0, x)
            out[w, s] = x.astype(jnp.bfloat16).reshape(2, BLK, C)
        return carry

    lax.fori_loop(0, (n + 1) // 2, project, 0)


def far_half(edges, flags, near, far_a, far_b, corner_a, corner_b, gain, w_qkv, w_out):
    k_near, vt_near, qt, spread, counts, peaks = near
    n = counts.shape[0] // 4
    return pl.pallas_call(
        functools.partial(far_kernel, edges, n),
        out_shape=jax.ShapeDtypeStruct((n, 2, 2, BLK, C), jnp.bfloat16),
        in_specs=[SMEM] * 3 + [VMEM] * 11,
        out_specs=VMEM,
        scratch_shapes=[
            pltpu.VMEM((2, 4, BLK, C), jnp.bfloat16),
            pltpu.VMEM((16, C), jnp.float32),
            pltpu.VMEM((2 * n, HALF, C), jnp.bfloat16),
            pltpu.VMEM((2 * n, C + ONES, HALF), jnp.bfloat16),
            pltpu.VMEM((C, C), jnp.bfloat16),
            pltpu.VMEM((C, C), jnp.bfloat16),
            pltpu.VMEM((8, BLK), jnp.float32),
            pltpu.VMEM((2, C, BLK), jnp.bfloat16),
            pltpu.VMEM((2 * n, C, HALF), jnp.bfloat16),
            pltpu.SMEM((2 * n,), jnp.int32),
        ],
        compiler_params=PARAMS,
        cost_estimate=pl.CostEstimate(flops=n * 10**9, bytes_accessed=n * 10**6, transcendentals=0),
        name="windows_edge" if edges else "windows_inner",
    )(flags, counts, peaks, far_a, far_b, corner_a, corner_b, gain, w_qkv, w_out, k_near, vt_near, qt, spread)


def permute(x, pairs):
    return lax.ppermute(x, ("lon", "lat"), pairs)


def shards(state, ocean_mask, norm_gain, w_qkv, w_out):
    lon_n, lat_n = lax.axis_size("lon"), lax.axis_size("lat")
    lat = lax.axis_index("lat")
    at = lambda i, j: i * lat_n + j
    every = [(i, j) for i in range(lon_n) for j in range(lat_n)]
    go_a = [(at(i, j), at(i, j - 1 if j % 2 else j + 1)) for i, j in every]
    go_b = [(at(i, j), at(i, j + 1 if j % 2 else j - 1)) for i, j in every if 0 < j < lat_n - 1]
    go_b += [(at(i, lat_n - 1), at(lon_n - 1 - i, lat_n - 1)) for i in range(lon_n)]
    go_east = [(at(i, j), at((i + 1) % lon_n, j)) for i, j in every]
    go_west = [(at(i, j), at((i - 1) % lon_n, j)) for i, j in every]

    flags = jnp.stack([lat == 0, lat == lat_n - 1, lat % 2 == 1]).astype(jnp.int32)
    west = permute(edge_parts(flags, state, ocean_mask, state.shape[2] - SHIFT), go_east)
    east = permute(edge_parts(flags, state, ocean_mask, 0), go_west)
    part_a, part_b = prep(flags, state, ocean_mask)
    far_a = permute(part_a, go_a)
    far_b = permute(part_b, go_b)

    gain = norm_gain[None, :]
    near = near_half(False, part_a, part_b, part_a, part_b, gain, w_qkv)
    near_edge = near_half(True, part_a, part_b, west, east, gain, w_qkv)
    west, east, near, near_edge = lax.optimization_barrier((west, east, near, near_edge))
    corner_a = permute(jnp.stack([west[0], east[0]]), go_a)
    corner_b = permute(jnp.stack([west[1], east[1]]), go_b)
    inner = far_half(False, flags, near, far_a, far_b, far_a, far_b, gain, w_qkv, w_out)
    inner, near_edge = lax.optimization_barrier((inner, near_edge))
    outer = far_half(True, flags, near_edge, far_a, far_b, corner_a, corner_b, gain, w_qkv, w_out)
    return finish(flags, state, inner, outer)


def solution(mesh):
    in_specs = (P(None, "lat", "lon", None), P(None, "lat", "lon"), P(), P(), P())
    out_specs = P(None, "lat", "lon", None)
    return jax.shard_map(shards, mesh=mesh, in_specs=in_specs, out_specs=out_specs, check_vma=False)
```

```python
import functools

import jax
import jax.numpy as jnp
from jax import lax
from jax.experimental import pallas as pl
from jax.experimental.pallas import tpu as pltpu
from jax.sharding import PartitionSpec as P

C = 256
HEADS = 8
HEAD = C // HEADS
W = 16
SHIFT = 8
LEV = 2
HALF = W * W * LEV // 2
BLK = HALF // 2
QB = 32
ONES = 16
SMALL = 160
RIM = 3
PREP_LIMIT = 52 * 1024 * 1024
LAND = 1024.0
SAFE_SQ = 60.0**2

VMEM = pl.BlockSpec(memory_space=pltpu.VMEM)
SMEM = pl.BlockSpec(memory_space=pltpu.SMEM)
ANY = pl.BlockSpec(memory_space=pl.ANY)
PARAMS = pltpu.CompilerParams(vmem_limit_bytes=36 * 1024 * 1024)


def dot_nt(a, b):
    return lax.dot_general(a, b, (((1,), (1,)), ((), ())), preferred_element_type=jnp.float32)


def dot_nn(a, b):
    return jnp.dot(a, b, preferred_element_type=jnp.float32)


def iota(shape, axis):
    return lax.broadcasted_iota(jnp.int32, shape, axis)


def one(condition):
    return jnp.where(condition, 1.0, 0.0).astype(jnp.bfloat16)


def ocean_ranks(halves, rows_n):
    channel, row = iota((rows_n, C), 1), iota((rows_n, C), 0)
    marks = None
    for i, half in enumerate(halves):
        part = dot_nt(one((channel == 0) & (row == i)), half)
        marks = part if marks is None else marks + part
    ocean = jnp.where(marks < LAND / 2, 1.0, 0.0)
    return dot_nn(ocean.astype(jnp.bfloat16), one(iota((C, C), 0) <= iota((C, C), 1))) * ocean


def packed_norm(tokens, ranks, count, size, gain):
    wanted = jnp.minimum(iota((size, 1), 0) + 1, count).astype(jnp.float32)
    packed = dot_nn(one(ranks == wanted), tokens)
    average = jnp.mean(packed, axis=1, keepdims=True)
    centred = packed - average
    spread_sq = jnp.mean(centred * centred, axis=1, keepdims=True)
    return (centred * lax.rsqrt(spread_sq + 1e-05) * gain).astype(jnp.bfloat16)


def valid_rows(x, count):
    return jnp.where(iota((x.shape[0], 1), 0) < count, x.astype(jnp.float32), 0.0).astype(jnp.bfloat16)


def valid_ones(count, size):
    return one(jnp.broadcast_to(iota((1, size), 1) < count, (ONES, size)))


def head_norms(keys, sums):
    return jnp.max(dot_nn((keys * keys).astype(jnp.bfloat16), sums), axis=0, keepdims=True)


def fill(keys, values, i, key, size):
    keys[i, size:, :] = jnp.broadcast_to(key[0:1].astype(jnp.float32), (HALF - size, C)).astype(jnp.bfloat16)
    values[i, :, size:] = jnp.zeros((C + ONES, HALF - size), jnp.bfloat16)


def prep_kernel(flags, state, mask, inner_a, inner_b, outer_a, outer_b, to_east, to_west, held, held_mask, sems):
    blocks = state.shape[2] // SHIFT
    cols = blocks * SHIFT
    half = SHIFT // 2
    rim = outer_a.shape[0] // 2
    chunks = [(s, level, g) for s in range(2) for level in range(LEV) for g in range(2)]
    copies = []
    for i, (s, level, g) in enumerate(chunks):
        start = jnp.where(flags[2] == s, SHIFT, 0) + half * g
        copies.append(pltpu.make_async_copy(state.at[level, pl.ds(start, half)], held.at[i], sems.at[i]))
        copies[-1].start()
    mask_copy = pltpu.make_async_copy(mask, held_mask, sems.at[len(chunks)])
    mask_copy.start()
    eye = one(iota((cols, cols), 0) == iota((cols, cols), 1))
    mask_copy.wait()
    by_column = [
        dot_nt(eye, held_mask[level].astype(jnp.float32).astype(jnp.bfloat16)).astype(jnp.bfloat16) for level in range(LEV)
    ]
    for i, (s, level, g) in enumerate(chunks):
        inner, outer = ((inner_a, outer_a), (inner_b, outer_b))[s]
        first = jnp.where(flags[2] == s, SHIFT, 0) + half * g
        copies[i].wait()
        for p in range(half // 2):
            pair = []
            for row in (2 * p, 2 * p + 1):
                chosen = one(iota((2 * SHIFT, BLK), 0) == first + row)
                ocean = dot_nn(by_column[level], chosen)
                ocean = jnp.concatenate([ocean, ocean], axis=1)
                pair.append(jnp.where(ocean > 0.5, held[i, row].astype(jnp.float32), LAND).reshape(blocks, SHIFT, C))
            both = jnp.concatenate(pair, axis=1).astype(jnp.bfloat16)
            at = pl.ds((BLK // 2) * level + SHIFT * (half * g + 2 * p), 2 * SHIFT)
            inner[:, at, :] = both[rim : blocks - rim]
            outer[:rim, at, :] = both[:rim]
            outer[rim:, at, :] = both[blocks - rim :]
            to_east[s, at, :] = both[blocks - 1]
            to_west[s, at, :] = both[0]


def prep(flags, state, mask, rim):
    blocks = state.shape[2] // SHIFT
    shape = lambda n: jax.ShapeDtypeStruct((n, BLK, C), jnp.bfloat16)
    return pl.pallas_call(
        prep_kernel,
        out_shape=(shape(blocks - 2 * rim),) * 2 + (shape(2 * rim),) * 2 + (shape(2),) * 2,
        in_specs=[SMEM, ANY, ANY],
        out_specs=(VMEM,) * 6,
        scratch_shapes=[
            pltpu.VMEM((2 * LEV * 2, SHIFT // 2, state.shape[2], C), jnp.bfloat16),
            pltpu.VMEM(mask.shape, jnp.int32),
            pltpu.SemaphoreType.DMA((2 * LEV * 2 + 1,)),
        ],
        compiler_params=pltpu.CompilerParams(vmem_limit_bytes=PREP_LIMIT),
        name="windows_prep",
    )(flags, state, mask)


def finish_kernel(flags, state, inner, outer, out):
    level, r = pl.program_id(0), pl.program_id(1)
    s = jnp.where(r == 1, flags[2], 1 - flags[2])
    blocks = state.shape[2] // SHIFT
    for p in range(SHIFT // 2):
        at = pl.multiple_of(level * (BLK // 2) + 2 * SHIFT * p, 2 * SHIFT)
        deltas = []
        for b in range(blocks):
            rim = (blocks - 2 * inner.shape[0]) // 2
            if b < rim:
                delta = outer[(b + 1) // 2, s, 0 if b == 0 else 1 - b % 2, pl.ds(at, 2 * SHIFT), :]
            elif b < blocks - rim:
                delta = inner[(b - rim) // 2, s, (b - rim) % 2, pl.ds(at, 2 * SHIFT), :]
            else:
                k = b - (blocks - rim)
                delta = outer[(rim + 1) // 2 + k // 2, s, k % 2, pl.ds(at, 2 * SHIFT), :]
            deltas.append(delta.astype(jnp.float32))
        for i in range(2):
            added = jnp.concatenate([d[SHIFT * i : SHIFT * i + SHIFT] for d in deltas], axis=0)
            out[0, 2 * p + i] = (state[0, 2 * p + i].astype(jnp.float32) + added).astype(jnp.bfloat16)


def finish(flags, state, inner, outer):
    levels, rows, cols, _ = state.shape
    block = pl.BlockSpec((1, SHIFT, cols, C), lambda l, r, flags: (l, r, 0, 0))
    whole = lambda x: pl.BlockSpec(x.shape, lambda l, r, flags: (0,) * x.ndim)
    return pl.pallas_call(
        finish_kernel,
        out_shape=jax.ShapeDtypeStruct(state.shape, state.dtype),
        grid_spec=pltpu.PrefetchScalarGridSpec(
            num_scalar_prefetch=1,
            grid=(levels, 2),
            in_specs=[block, pl.BlockSpec(memory_space=pltpu.VMEM), pl.BlockSpec(memory_space=pltpu.VMEM)],
            out_specs=block,
        ),
        compiler_params=PARAMS,
        name="windows_finish",
    )(flags, state, inner, outer)


def pairs_of(j, n):
    return [(w, s) for w in (2 * j, jnp.minimum(2 * j + 1, n - 1)) for s in range(2)]


def near_kernel(edges, n, part_a, part_b, gain, w_qkv, k_out, vt_out, qt_out, spread_out, counts, peaks, ranks, wqt, wvt, norms):
    parts = (part_a, part_b)

    def tokens_at(w, s):
        return parts[s][pl.ds(2 * w, 2)].reshape(HALF, C)

    rank = ocean_ranks([tokens_at(i // 2, i % 2) for i in range(2 * n)], 16)
    ranks[...] = rank
    for i in range(2 * n):
        counts[i] = jnp.max(rank[i : i + 1, :]).astype(jnp.int32)
        is_edge = edges and i // 2 in (0, n - 1)
        counts[2 * n + i] = jnp.max(rank[i : i + 1, :BLK]).astype(jnp.int32) if is_edge else counts[i]

    eye = one(iota((C, C), 0) == iota((C, C), 1))
    wqt[...] = dot_nt(eye, w_qkv[:, :C]).astype(jnp.bfloat16)
    wvt[...] = dot_nt(eye, w_qkv[:, 2 * C :]).astype(jnp.bfloat16)
    norms[...] = jnp.zeros_like(norms)
    by_column = dot_nt(eye, rank.astype(jnp.bfloat16)).astype(jnp.bfloat16)
    for i in range(2 * n):
        col_rank = dot_nn(by_column, one(iota((16, BLK), 0) == i))
        for at in (0, BLK):
            number = (iota((HALF, BLK), 1) + (at + 1)).astype(jnp.float32)
            spread_out[i, :, at : at + BLK] = one(col_rank == number)

    def window(size, j):
        sums = one(iota((C, BLK), 0) // HEAD == iota((C, BLK), 1))
        sums_t = one(iota((ONES, C), 1) // HEAD == iota((ONES, C), 0))
        items = pairs_of(j, n)
        count = [counts[2 * w + s] for w, s in items]
        normed = [
            packed_norm(tokens_at(w, s), ranks[pl.ds(2 * w + s, 1), :], c, size, gain[...]) for (w, s), c in zip(items, count)
        ]
        keys = [dot_nn(x, w_qkv[:, C : 2 * C]).astype(jnp.bfloat16) for x in normed]
        queries = [(dot_nt(wqt[...], x) * (1.0 / HEAD**0.5)).astype(jnp.bfloat16) for x in normed]
        values = [dot_nt(wvt[...], valid_rows(x, c)).astype(jnp.bfloat16) for x, c in zip(normed, count)]
        for (w, s), c, key, query, value in zip(items, count, keys, queries, values):
            k_out[2 * w + s, :size, :] = key
            qt_out[2 * w + s, :, :size] = query
            vt_out[2 * w + s, :C, :size] = value
            vt_out[2 * w + s, C:, :size] = valid_ones(c, size)
            if size < HALF:
                qt_out[2 * w + s, :, size:] = jnp.zeros((C, HALF - size), jnp.bfloat16)
                fill(k_out, vt_out, 2 * w + s, key, size)
            norms[0:1, :] = jnp.maximum(norms[0:1, :], head_norms(key, sums))
            by_head = dot_nn(sums_t, query * query)
            norms[8:, :] = jnp.maximum(norms[8:, :], jnp.max(by_head, axis=1, keepdims=True))

    def either(j, carry):
        largest = functools.reduce(jnp.maximum, [counts[2 * w + s] for w, s in pairs_of(j, n)])
        for size, fits in ((SMALL, largest <= SMALL), (HALF, largest > SMALL)):
            pl.when(fits)(functools.partial(window, size, j))
        return carry

    lax.fori_loop(0, (n + 1) // 2, either, 0)
    peaks[0] = jnp.max(norms[0:1, :])
    peaks[1] = jnp.max(norms[8:, :])


def near_half(edges, part_a, part_b, gain, w_qkv):
    n = part_a.shape[0] // 2
    bf = lambda *shape: jax.ShapeDtypeStruct(shape, jnp.bfloat16)
    return pl.pallas_call(
        functools.partial(near_kernel, edges, n),
        out_shape=(
            bf(2 * n, HALF, C),
            bf(2 * n, C + ONES, HALF),
            bf(2 * n, C, HALF),
            bf(2 * n, HALF, HALF),
            jax.ShapeDtypeStruct((4 * n,), jnp.int32),
            jax.ShapeDtypeStruct((2,), jnp.float32),
        ),
        in_specs=[VMEM] * 4,
        out_specs=(VMEM,) * 4 + (SMEM,) * 2,
        scratch_shapes=[
            pltpu.VMEM((16, C), jnp.float32),
            pltpu.VMEM((C, C), jnp.bfloat16),
            pltpu.VMEM((C, C), jnp.bfloat16),
            pltpu.VMEM((8 + ONES, BLK), jnp.float32),
        ],
        compiler_params=PARAMS,
        cost_estimate=pl.CostEstimate(flops=n * 10**9, bytes_accessed=n * 10**6, transcendentals=0),
        name="windows_near_edge" if edges else "windows_near",
    )(part_a, part_b, gain, w_qkv)


def tops(scores, bounded):
    if bounded:
        return scores
    top = jnp.maximum(jnp.max(scores[0], axis=0, keepdims=True), jnp.max(scores[1], axis=0, keepdims=True))
    return [score - top for score in scores]


def mix(scores, values, slots, queries_n):
    parts = [dot_nn(value, jnp.exp(score).astype(jnp.bfloat16)) for score, value in zip(scores, values)]
    summed = parts[0] + parts[1]
    n = summed.shape[0] - ONES
    total = summed[n : n + 1, :] + jnp.where(slots < queries_n, 0.0, 1.0)
    return summed[:n, :] * (1.0 / total)


def far_kernel(
    n, flags, counts, peaks, far_a, far_b, gain, w_qkv, w_out, k_near, vt_near, qt, spread, out,
    ranks, k_far, vt_far, wvt, woutt, norms, mixes, count_far,
):
    far_refs = (far_a, far_b)

    def tokens_at(w, s):
        i = jnp.where(flags[1] == 1, n - 1 - w, w) if s == 1 else w
        return far_refs[s][pl.ds(2 * i, 2)].reshape(HALF, C)

    rank = ocean_ranks([tokens_at(i // 2, i % 2) for i in range(2 * n)], 16)
    ranks[...] = rank
    for i in range(2 * n):
        found = jnp.max(rank[i : i + 1, :]).astype(jnp.int32)
        count_far[i] = jnp.where(flags[0] == 1, 0, found) if i % 2 else found
    eye = one(iota((C, C), 0) == iota((C, C), 1))
    wvt[...] = dot_nt(eye, w_qkv[:, 2 * C :]).astype(jnp.bfloat16)
    woutt[...] = dot_nt(eye, w_out[...]).astype(jnp.bfloat16)
    norms[...] = jnp.zeros_like(norms)

    def prepare(size, j):
        sums = one(iota((C, BLK), 0) // HEAD == iota((C, BLK), 1))
        items = pairs_of(j, n)
        count = [count_far[2 * w + s] for w, s in items]
        normed = [
            packed_norm(tokens_at(w, s), ranks[pl.ds(2 * w + s, 1), :], c, size, gain[...]) for (w, s), c in zip(items, count)
        ]
        keys = [dot_nn(x, w_qkv[:, C : 2 * C]).astype(jnp.bfloat16) for x in normed]
        values = [dot_nt(wvt[...], valid_rows(x, c)).astype(jnp.bfloat16) for x, c in zip(normed, count)]
        for (w, s), c, key, value in zip(items, count, keys, values):
            k_far[2 * w + s, :size, :] = key
            vt_far[2 * w + s, :C, :size] = value
            vt_far[2 * w + s, C:, :size] = valid_ones(c, size)
            if size < HALF:
                fill(k_far, vt_far, 2 * w + s, key, size)
            norms[0:1, :] = jnp.maximum(norms[0:1, :], head_norms(key, sums))

    def ready(j, carry):
        largest = functools.reduce(jnp.maximum, [count_far[2 * w + s] for w, s in pairs_of(j, n)])
        for size, fits in ((SMALL, largest <= SMALL), (HALF, largest > SMALL)):
            pl.when(fits)(functools.partial(prepare, size, j))
        return carry

    lax.fori_loop(0, (n + 1) // 2, ready, 0)
    peak = jnp.maximum(jnp.max(norms[0:1, :]), peaks[0]) * peaks[1]
    safe = peak <= SAFE_SQ

    lane = iota((1, C), 1)

    def attend(w, halves, size, bounded):
        asked = {s: counts[2 * n + 2 * w + s] for s in halves}
        at = {s: 2 * w + s for s in halves}
        keys = {s: [k_near[at[s], :size, :], k_far[2 * w + s, :size, :]] for s in halves}
        if not bounded:
            for s in halves:
                near, far = [key.astype(jnp.float32) for key in keys[s]]
                far = jnp.where(count_far[2 * w + s] > 0, far, jnp.broadcast_to(near[0:1], far.shape))
                keys[s][1] = far.astype(jnp.bfloat16)

        def values(s, rows):
            return [
                jnp.concatenate([ref[i, rows, :size], ref[i, C : C + ONES, :size]], axis=0)
                for ref, i in ((vt_near, at[s]), (vt_far, 2 * w + s))
            ]

        def base_scores(t, s):
            g = t // 2
            none = jnp.zeros((HEAD, BLK), jnp.bfloat16)
            rows = []
            for h in range(4 * g, 4 * g + 4):
                mine = qt[at[s], HEAD * h : HEAD * h + HEAD, :BLK] if h // 2 == t else none
                rows.append(jnp.concatenate([mine, none] if h % 2 == 0 else [none, mine], axis=1))
            stacked = jnp.concatenate(rows, axis=0)
            return [dot_nn(key[:, BLK * g : BLK * g + BLK], stacked) for key in keys[s]]

        sub, lan = iota((C, C), 0), iota((C, C), 1)
        block = sub // HEAD == lan // QB

        def rest_stacked(start, s):
            repeat = one(sub[:BLK] + BLK == start + lan[:BLK] % QB)
            return jnp.where(block, dot_nn(qt[at[s], :, BLK:], repeat), 0.0).astype(jnp.bfloat16)

        def rest_mixed(start, s, scores):
            mixed = mix(tops(scores, bounded), values(s, slice(0, C)), start + lane % QB, asked[s])
            mixed = jnp.where(block, mixed, 0.0).astype(jnp.bfloat16)
            return dot_nn(mixed, one(sub[:, :BLK] % QB + start == lan[:, :BLK] + BLK))

        tiles = [(t, s) for t in range(4) for s in halves]
        ahead = base_scores(*tiles[0])
        for i, (t, s) in enumerate(tiles):
            now = ahead
            if i + 1 < len(tiles):
                ahead = base_scores(*tiles[i + 1])
            mixed = mix(tops(now, bounded), values(s, slice(64 * t, 64 * t + 64)), lane % BLK, asked[s])
            mixes[2 * w + s, 64 * t : 64 * t + HEAD, :BLK] = mixed[:HEAD, :BLK].astype(jnp.bfloat16)
            mixes[2 * w + s, 64 * t + HEAD : 64 * t + 64, :BLK] = mixed[HEAD:, BLK:].astype(jnp.bfloat16)
        for s in halves:
            mixes[2 * w + s, :, BLK:] = jnp.zeros((C, BLK), jnp.bfloat16)

        most = functools.reduce(jnp.maximum, asked.values())

        def more(b, carry):
            start = b * QB
            stacked = [rest_stacked(start, s) for s in halves]
            scores = [[dot_nn(key, x) for key in keys[s]] for s, x in zip(halves, stacked)]
            placed = [rest_mixed(start, s, score) for s, score in zip(halves, scores)]
            for s, x in zip(halves, placed):
                mixes[2 * w + s, :, BLK:] = (mixes[2 * w + s, :, BLK:].astype(jnp.float32) + x).astype(jnp.bfloat16)
            return carry

        def rest():
            none = jnp.zeros((HEAD, BLK), jnp.float32)
            stacked = []
            for s in halves:
                rows = []
                for h in range(HEADS):
                    x = qt[at[s], HEAD * h : HEAD * h + HEAD, BLK:].astype(jnp.float32)
                    x = pltpu.roll(x, QB * (h % 4), 1) if h % 4 else x
                    rows.append(jnp.concatenate([x, none] if h < 4 else [none, x], axis=1))
                stacked.append(jnp.concatenate(rows, axis=0).astype(jnp.bfloat16))
            scores = [[dot_nn(key, x) for key in keys[s]] for s, x in zip(halves, stacked)]
            mixed = [
                mix(tops(score, bounded), values(s, slice(0, C)), BLK + lane % QB, asked[s]) for s, score in zip(halves, scores)
            ]
            for s, x in zip(halves, mixed):
                for h in range(HEADS):
                    piece = x[HEAD * h : HEAD * h + HEAD, BLK * (h // 4) : BLK * (h // 4) + BLK]
                    piece = pltpu.roll(piece, BLK - QB * (h % 4), 1) if h % 4 else piece
                    piece = jnp.where(iota((HEAD, BLK), 1) < QB, piece, 0.0)
                    mixes[2 * w + s, HEAD * h : HEAD * h + HEAD, BLK:] = piece.astype(jnp.bfloat16)

        if size <= BLK + QB:
            pl.when(most > BLK)(rest)
        else:
            lax.fori_loop(BLK // QB, (most + QB - 1) // QB, more, 0)

    def window(w, carry):
        at = 2 * w
        largest = jnp.maximum(jnp.maximum(counts[at], counts[at + 1]), jnp.maximum(count_far[2 * w], count_far[2 * w + 1]))
        active = jnp.maximum(counts[2 * n + at], counts[2 * n + at + 1]) > 0

        @pl.when(jnp.logical_not(active))
        def _():
            for s in range(2):
                mixes[2 * w + s] = jnp.zeros_like(mixes[2 * w + s])

        pl.when(active & safe & (largest <= SMALL))(functools.partial(attend, w, (0, 1), SMALL, True))
        pl.when(active & safe & (largest > SMALL))(functools.partial(attend, w, (0, 1), HALF, True))
        for s in range(2):
            pl.when(active & jnp.logical_not(safe))(functools.partial(attend, w, (s,), HALF, False))
        return carry

    lax.fori_loop(0, n, window, 0)

    def project(j, carry):
        items = pairs_of(j, n)
        delta_t = [dot_nn(woutt[...], mixes[2 * w + s]).astype(jnp.bfloat16) for w, s in items]
        delta = [dot_nt(spread[2 * w + s], x) for (w, s), x in zip(items, delta_t)]
        for (w, s), x in zip(items, delta):
            if s == 1:
                x = jnp.where(flags[0] == 1, 0.0, x)
            out[w, s] = x.astype(jnp.bfloat16).reshape(2, BLK, C)
        return carry

    lax.fori_loop(0, (n + 1) // 2, project, 0)


def far_half(edges, flags, near, far_a, far_b, gain, w_qkv, w_out):
    k_near, vt_near, qt, spread, counts, peaks = near
    n = counts.shape[0] // 4
    return pl.pallas_call(
        functools.partial(far_kernel, n),
        out_shape=jax.ShapeDtypeStruct((n, 2, 2, BLK, C), jnp.bfloat16),
        in_specs=[SMEM] * 3 + [VMEM] * 9,
        out_specs=VMEM,
        scratch_shapes=[
            pltpu.VMEM((16, C), jnp.float32),
            pltpu.VMEM((2 * n, HALF, C), jnp.bfloat16),
            pltpu.VMEM((2 * n, C + ONES, HALF), jnp.bfloat16),
            pltpu.VMEM((C, C), jnp.bfloat16),
            pltpu.VMEM((C, C), jnp.bfloat16),
            pltpu.VMEM((8, BLK), jnp.float32),
            pltpu.VMEM((2 * n, C, HALF), jnp.bfloat16),
            pltpu.SMEM((2 * n,), jnp.int32),
        ],
        compiler_params=PARAMS,
        cost_estimate=pl.CostEstimate(flops=n * 10**9, bytes_accessed=n * 10**6, transcendentals=0),
        name="windows_edge" if edges else "windows_inner",
    )(flags, counts, peaks, far_a, far_b, gain, w_qkv, w_out, k_near, vt_near, qt, spread)


def permute(x, pairs):
    return lax.ppermute(x, ("lon", "lat"), pairs)


def shards(state, ocean_mask, norm_gain, w_qkv, w_out):
    lon_n, lat_n = lax.axis_size("lon"), lax.axis_size("lat")
    lat = lax.axis_index("lat")
    at = lambda i, j: i * lat_n + j
    every = [(i, j) for i in range(lon_n) for j in range(lat_n)]
    go_a = [(at(i, j), at(i, j - 1 if j % 2 else j + 1)) for i, j in every]
    go_b = [(at(i, j), at(i, j + 1 if j % 2 else j - 1)) for i, j in every if 0 < j < lat_n - 1]
    go_b += [(at(i, lat_n - 1), at(lon_n - 1 - i, lat_n - 1)) for i in range(lon_n)]
    go_east = [(at(i, j), at((i + 1) % lon_n, j)) for i, j in every]
    go_west = [(at(i, j), at((i - 1) % lon_n, j)) for i, j in every]

    flags = jnp.stack([lat == 0, lat == lat_n - 1, lat % 2 == 1]).astype(jnp.int32)
    inner_a, inner_b, outer_a, outer_b, to_east, to_west = prep(flags, state, ocean_mask, RIM)
    west = permute(to_east, go_east)
    east = permute(to_west, go_west)
    far_a = permute(inner_a, go_a)
    far_b = permute(inner_b, go_b)
    rim = lambda x, s: jnp.concatenate([x[:1], west[s : s + 1], x[1:], east[s : s + 1]])
    outer_a, outer_b = rim(outer_a, 0), rim(outer_b, 1)
    rim_a = permute(outer_a, go_a)
    rim_b = permute(outer_b, go_b)

    gain = norm_gain[None, :]
    near = near_half(False, inner_a, inner_b, gain, w_qkv)
    near_rim = near_half(True, outer_a, outer_b, gain, w_qkv)
    near, near_rim = lax.optimization_barrier((near, near_rim))
    inner = far_half(False, flags, near, far_a, far_b, gain, w_qkv, w_out)
    inner, near_rim = lax.optimization_barrier((inner, near_rim))
    outer = far_half(True, flags, near_rim, rim_a, rim_b, gain, w_qkv, w_out)
    return finish(flags, state, inner, outer)


def solution(mesh):
    in_specs = (P(None, "lat", "lon", None), P(None, "lat", "lon"), P(), P(), P())
    out_specs = P(None, "lat", "lon", None)
    return jax.shard_map(shards, mesh=mesh, in_specs=in_specs, out_specs=out_specs, check_vma=False)
```

```python
import functools

import jax
import jax.numpy as jnp
from jax import lax
from jax.experimental import pallas as pl
from jax.experimental.pallas import tpu as pltpu
from jax.sharding import PartitionSpec as P

C = 256
HEADS = 8
HEAD = C // HEADS
W = 16
SHIFT = 8
LEV = 2
HALF = W * W * LEV // 2
BLK = HALF // 2
QB = 32
ONES = 16
SIZES = (144, 176)
GROUP = 4
RIM = 3
LAND = 1024.0
SAFE_SQ = 60.0**2

VMEM = pl.BlockSpec(memory_space=pltpu.VMEM)
SMEM = pl.BlockSpec(memory_space=pltpu.SMEM)
ANY = pl.BlockSpec(memory_space=pl.ANY)
PARAMS = pltpu.CompilerParams(vmem_limit_bytes=36 * 1024 * 1024)


def dot_nt(a, b):
    return lax.dot_general(a, b, (((1,), (1,)), ((), ())), preferred_element_type=jnp.float32)


def dot_nn(a, b):
    return jnp.dot(a, b, preferred_element_type=jnp.float32)


def iota(shape, axis):
    return lax.broadcasted_iota(jnp.int32, shape, axis)


def one(condition):
    return jnp.where(condition, 1.0, 0.0).astype(jnp.bfloat16)


def ocean_ranks(halves, rows_n):
    channel, row = iota((rows_n, C), 1), iota((rows_n, C), 0)
    marks = None
    for i, half in enumerate(halves):
        part = dot_nt(one((channel == 0) & (row == i)), half)
        marks = part if marks is None else marks + part
    ocean = jnp.where(marks < LAND / 2, 1.0, 0.0)
    return dot_nn(ocean.astype(jnp.bfloat16), one(iota((C, C), 0) <= iota((C, C), 1))) * ocean


def packed_norm(tokens, ranks, count, size, gain):
    wanted = jnp.minimum(iota((size, 1), 0) + 1, count).astype(jnp.float32)
    packed = dot_nn(one(ranks == wanted), tokens)
    average = jnp.mean(packed, axis=1, keepdims=True)
    centred = packed - average
    spread_sq = jnp.mean(centred * centred, axis=1, keepdims=True)
    return (centred * lax.rsqrt(spread_sq + 1e-05) * gain).astype(jnp.bfloat16)


def valid_rows(x, count):
    return jnp.where(iota((x.shape[0], 1), 0) < count, x.astype(jnp.float32), 0.0).astype(jnp.bfloat16)


def valid_ones(count, size):
    return one(jnp.broadcast_to(iota((1, size), 1) < count, (ONES, size)))


def head_norms(keys, sums):
    return jnp.max(dot_nn((keys * keys).astype(jnp.bfloat16), sums), axis=0, keepdims=True)


def fill(keys, values, i, key, size):
    keys[i, size:, :] = jnp.broadcast_to(key[0:1].astype(jnp.float32), (HALF - size, C)).astype(jnp.bfloat16)
    values[i, :, size:] = jnp.zeros((C + ONES, HALF - size), jnp.bfloat16)


def prep_kernel(flags, state, mask, inner_a, inner_b, outer_a, outer_b, to_east, to_west):
    blocks = state.shape[2] // SHIFT
    cols = blocks * SHIFT
    rim = outer_a.shape[0] // 2
    eye = one(iota((cols, cols), 0) == iota((cols, cols), 1))
    by_column = [dot_nt(eye, mask[level]).astype(jnp.bfloat16) for level in range(LEV)]
    for s, inner, outer in ((0, inner_a, outer_a), (1, inner_b, outer_b)):
        first = jnp.where(flags[2] == s, SHIFT, 0)
        for level in range(LEV):
            for p in range(SHIFT // 2):
                pair = []
                for row in (2 * p, 2 * p + 1):
                    chosen = one(iota((2 * SHIFT, BLK), 0) == first + row)
                    ocean = dot_nn(by_column[level], chosen)
                    ocean = jnp.concatenate([ocean, ocean], axis=1)
                    values = state[level, first + row].astype(jnp.float32)
                    pair.append(jnp.where(ocean > 0.5, values, LAND).reshape(blocks, SHIFT, C))
                both = jnp.concatenate(pair, axis=1).astype(jnp.bfloat16)
                at = pl.ds((BLK // 2) * level + 2 * SHIFT * p, 2 * SHIFT)
                inner[:, at, :] = both[rim : blocks - rim]
                outer[:rim, at, :] = both[:rim]
                outer[rim:, at, :] = both[blocks - rim :]
                to_east[s, at, :] = both[blocks - 1]
                to_west[s, at, :] = both[0]


def prep(flags, state, mask, rim):
    blocks = state.shape[2] // SHIFT
    shape = lambda n: jax.ShapeDtypeStruct((n, BLK, C), jnp.bfloat16)
    return pl.pallas_call(
        prep_kernel,
        out_shape=(shape(blocks - 2 * rim),) * 2 + (shape(2 * rim),) * 2 + (shape(2),) * 2,
        in_specs=[SMEM, VMEM, VMEM],
        out_specs=(VMEM,) * 6,
        compiler_params=PARAMS,
        name="windows_prep",
    )(flags, state, mask.astype(jnp.bfloat16))


def finish_kernel(flags, state, inner, outer, out):
    level, r = pl.program_id(0), pl.program_id(1)
    s = jnp.where(r == 1, flags[2], 1 - flags[2])
    blocks = state.shape[2] // SHIFT
    for p in range(SHIFT // 2):
        at = pl.multiple_of(level * (BLK // 2) + 2 * SHIFT * p, 2 * SHIFT)
        deltas = []
        for b in range(blocks):
            rim = (blocks - 2 * inner.shape[0]) // 2
            if b < rim:
                delta = outer[(b + 1) // 2, s, 0 if b == 0 else 1 - b % 2, pl.ds(at, 2 * SHIFT), :]
            elif b < blocks - rim:
                delta = inner[(b - rim) // 2, s, (b - rim) % 2, pl.ds(at, 2 * SHIFT), :]
            else:
                k = b - (blocks - rim)
                delta = outer[(rim + 1) // 2 + k // 2, s, k % 2, pl.ds(at, 2 * SHIFT), :]
            deltas.append(delta.astype(jnp.float32))
        for i in range(2):
            added = jnp.concatenate([d[SHIFT * i : SHIFT * i + SHIFT] for d in deltas], axis=0)
            out[0, 2 * p + i] = (state[0, 2 * p + i].astype(jnp.float32) + added).astype(jnp.bfloat16)


def finish(flags, state, inner, outer):
    levels, rows, cols, _ = state.shape
    block = pl.BlockSpec((1, SHIFT, cols, C), lambda l, r, flags: (l, r, 0, 0))
    whole = lambda x: pl.BlockSpec(x.shape, lambda l, r, flags: (0,) * x.ndim)
    return pl.pallas_call(
        finish_kernel,
        out_shape=jax.ShapeDtypeStruct(state.shape, state.dtype),
        grid_spec=pltpu.PrefetchScalarGridSpec(
            num_scalar_prefetch=1,
            grid=(levels, 2),
            in_specs=[block, pl.BlockSpec(memory_space=pltpu.VMEM), pl.BlockSpec(memory_space=pltpu.VMEM)],
            out_specs=block,
        ),
        compiler_params=PARAMS,
        name="windows_finish",
    )(flags, state, inner, outer)


def by_size(n, counts, work):
    largest = functools.reduce(jnp.maximum, [counts[i] for i in range(2 * n)])
    items = [(i // 2, i % 2) for i in range(2 * n)]
    under = 0
    for size in SIZES:

        @pl.when((largest > under) & (largest <= size) if under else largest <= size)
        def _(size=size):
            for i in range(0, 2 * n, GROUP):
                work(size, items[i : i + GROUP])

        under = size

    @pl.when(largest > under)
    def _():
        def step(w, carry):
            work(HALF, [(w, 0), (w, 1)])
            return carry

        lax.fori_loop(0, n, step, 0)


def near_kernel(edges, n, part_a, part_b, gain, w_qkv, k_out, vt_out, qt_out, spread_out, counts, peaks, ranks, wqt, wvt, norms):
    parts = (part_a, part_b)

    def tokens_at(w, s):
        return parts[s][pl.ds(2 * w, 2)].reshape(HALF, C)

    rank = ocean_ranks([tokens_at(i // 2, i % 2) for i in range(2 * n)], 16)
    ranks[...] = rank
    for i in range(2 * n):
        counts[i] = jnp.max(rank[i : i + 1, :]).astype(jnp.int32)
        is_edge = edges and i // 2 in (0, n - 1)
        counts[2 * n + i] = jnp.max(rank[i : i + 1, :BLK]).astype(jnp.int32) if is_edge else counts[i]

    eye = one(iota((C, C), 0) == iota((C, C), 1))
    wqt[...] = dot_nt(eye, w_qkv[:, :C]).astype(jnp.bfloat16)
    wvt[...] = dot_nt(eye, w_qkv[:, 2 * C :]).astype(jnp.bfloat16)
    norms[...] = jnp.zeros_like(norms)
    by_column = dot_nt(eye, rank.astype(jnp.bfloat16)).astype(jnp.bfloat16)
    for i in range(2 * n):
        col_rank = dot_nn(by_column, one(iota((16, BLK), 0) == i))
        for at in (0, BLK):
            number = (iota((HALF, BLK), 1) + (at + 1)).astype(jnp.float32)
            spread_out[i, :, at : at + BLK] = one(col_rank == number)

    def window(size, items):
        sums = one(iota((C, BLK), 0) // HEAD == iota((C, BLK), 1))
        sums_t = one(iota((ONES, C), 1) // HEAD == iota((ONES, C), 0))
        count = [counts[2 * w + s] for w, s in items]
        normed = [
            packed_norm(tokens_at(w, s), ranks[pl.ds(2 * w + s, 1), :], c, size, gain[...]) for (w, s), c in zip(items, count)
        ]
        keys = [dot_nn(x, w_qkv[:, C : 2 * C]).astype(jnp.bfloat16) for x in normed]
        queries = [(dot_nt(wqt[...], x) * (1.0 / HEAD**0.5)).astype(jnp.bfloat16) for x in normed]
        values = [dot_nt(wvt[...], valid_rows(x, c)).astype(jnp.bfloat16) for x, c in zip(normed, count)]
        for (w, s), c, key, query, value in zip(items, count, keys, queries, values):
            k_out[2 * w + s, :size, :] = key
            qt_out[2 * w + s, :, :size] = query
            vt_out[2 * w + s, :C, :size] = value
            vt_out[2 * w + s, C:, :size] = valid_ones(c, size)
            if size < HALF:
                qt_out[2 * w + s, :, size:] = jnp.zeros((C, HALF - size), jnp.bfloat16)
                fill(k_out, vt_out, 2 * w + s, key, size)
            norms[0:1, :] = jnp.maximum(norms[0:1, :], head_norms(key, sums))
            by_head = dot_nn(sums_t, query * query)
            norms[8:, :] = jnp.maximum(norms[8:, :], jnp.max(by_head, axis=1, keepdims=True))

    by_size(n, counts, window)
    peaks[0] = jnp.max(norms[0:1, :])
    peaks[1] = jnp.max(norms[8:, :])


def near_half(edges, part_a, part_b, gain, w_qkv):
    n = part_a.shape[0] // 2
    bf = lambda *shape: jax.ShapeDtypeStruct(shape, jnp.bfloat16)
    return pl.pallas_call(
        functools.partial(near_kernel, edges, n),
        out_shape=(
            bf(2 * n, HALF, C),
            bf(2 * n, C + ONES, HALF),
            bf(2 * n, C, HALF),
            bf(2 * n, HALF, HALF),
            jax.ShapeDtypeStruct((4 * n,), jnp.int32),
            jax.ShapeDtypeStruct((2,), jnp.float32),
        ),
        in_specs=[VMEM] * 4,
        out_specs=(VMEM,) * 4 + (SMEM,) * 2,
        scratch_shapes=[
            pltpu.VMEM((16, C), jnp.float32),
            pltpu.VMEM((C, C), jnp.bfloat16),
            pltpu.VMEM((C, C), jnp.bfloat16),
            pltpu.VMEM((8 + ONES, BLK), jnp.float32),
        ],
        compiler_params=PARAMS,
        cost_estimate=pl.CostEstimate(flops=n * 10**9, bytes_accessed=n * 10**6, transcendentals=0),
        name="windows_near_edge" if edges else "windows_near",
    )(part_a, part_b, gain, w_qkv)


def tops(scores, bounded):
    if bounded:
        return scores
    top = jnp.maximum(jnp.max(scores[0], axis=0, keepdims=True), jnp.max(scores[1], axis=0, keepdims=True))
    return [score - top for score in scores]


def mix(scores, values, slots, queries_n):
    parts = [dot_nn(value, jnp.exp(score).astype(jnp.bfloat16)) for score, value in zip(scores, values)]
    summed = parts[0] + parts[1]
    n = summed.shape[0] - ONES
    total = summed[n : n + 1, :] + jnp.where(slots < queries_n, 0.0, 1.0)
    return summed[:n, :] * (1.0 / total)


def far_kernel(
    n, flags, counts, peaks, far_a, far_b, gain, w_qkv, w_out, k_near, vt_near, qt, spread, out,
    ranks, k_far, vt_far, wvt, woutt, norms, mixes, count_far,
):
    far_refs = (far_a, far_b)

    def tokens_at(w, s):
        i = jnp.where(flags[1] == 1, n - 1 - w, w) if s == 1 else w
        return far_refs[s][pl.ds(2 * i, 2)].reshape(HALF, C)

    rank = ocean_ranks([tokens_at(i // 2, i % 2) for i in range(2 * n)], 16)
    ranks[...] = rank
    for i in range(2 * n):
        found = jnp.max(rank[i : i + 1, :]).astype(jnp.int32)
        count_far[i] = jnp.where(flags[0] == 1, 0, found) if i % 2 else found
    eye = one(iota((C, C), 0) == iota((C, C), 1))
    wvt[...] = dot_nt(eye, w_qkv[:, 2 * C :]).astype(jnp.bfloat16)
    woutt[...] = dot_nt(eye, w_out[...]).astype(jnp.bfloat16)
    norms[...] = jnp.zeros_like(norms)

    def prepare(size, items):
        sums = one(iota((C, BLK), 0) // HEAD == iota((C, BLK), 1))
        count = [count_far[2 * w + s] for w, s in items]
        normed = [
            packed_norm(tokens_at(w, s), ranks[pl.ds(2 * w + s, 1), :], c, size, gain[...]) for (w, s), c in zip(items, count)
        ]
        keys = [dot_nn(x, w_qkv[:, C : 2 * C]).astype(jnp.bfloat16) for x in normed]
        values = [dot_nt(wvt[...], valid_rows(x, c)).astype(jnp.bfloat16) for x, c in zip(normed, count)]
        for (w, s), c, key, value in zip(items, count, keys, values):
            k_far[2 * w + s, :size, :] = key
            vt_far[2 * w + s, :C, :size] = value
            vt_far[2 * w + s, C:, :size] = valid_ones(c, size)
            if size < HALF:
                fill(k_far, vt_far, 2 * w + s, key, size)
            norms[0:1, :] = jnp.maximum(norms[0:1, :], head_norms(key, sums))

    by_size(n, count_far, prepare)
    peak = jnp.maximum(jnp.max(norms[0:1, :]), peaks[0]) * peaks[1]
    safe = peak <= SAFE_SQ

    lane = iota((1, C), 1)

    def attend(w, halves, size, bounded):
        at = {k: 2 * w + s for k, s in halves.items()}
        asked = {k: counts[2 * n + i] for k, i in at.items()}
        keys = {s: [k_near[at[s], :size, :], k_far[at[s], :size, :]] for s in halves}
        if not bounded:
            for s in halves:
                near, far = [key.astype(jnp.float32) for key in keys[s]]
                far = jnp.where(count_far[at[s]] > 0, far, jnp.broadcast_to(near[0:1], far.shape))
                keys[s][1] = far.astype(jnp.bfloat16)

        def values(s, rows):
            return [
                jnp.concatenate([ref[i, rows, :size], ref[i, C : C + ONES, :size]], axis=0)
                for ref, i in ((vt_near, at[s]), (vt_far, at[s]))
            ]

        def base_scores(t, s):
            g = t // 2
            none = jnp.zeros((HEAD, BLK), jnp.bfloat16)
            rows = []
            for h in range(4 * g, 4 * g + 4):
                mine = qt[at[s], HEAD * h : HEAD * h + HEAD, :BLK] if h // 2 == t else none
                rows.append(jnp.concatenate([mine, none] if h % 2 == 0 else [none, mine], axis=1))
            stacked = jnp.concatenate(rows, axis=0)
            return [dot_nn(key[:, BLK * g : BLK * g + BLK], stacked) for key in keys[s]]

        sub, lan = iota((C, C), 0), iota((C, C), 1)
        block = sub // HEAD == lan // QB

        def rest_stacked(start, s):
            repeat = one(sub[:BLK] + BLK == start + lan[:BLK] % QB)
            return jnp.where(block, dot_nn(qt[at[s], :, BLK:], repeat), 0.0).astype(jnp.bfloat16)

        def rest_mixed(start, s, scores):
            mixed = mix(tops(scores, bounded), values(s, slice(0, C)), start + lane % QB, asked[s])
            mixed = jnp.where(block, mixed, 0.0).astype(jnp.bfloat16)
            return dot_nn(mixed, one(sub[:, :BLK] % QB + start == lan[:, :BLK] + BLK))

        tiles = [(t, s) for t in range(4) for s in halves]
        ahead = base_scores(*tiles[0])
        for i, (t, s) in enumerate(tiles):
            now = ahead
            if i + 1 < len(tiles):
                ahead = base_scores(*tiles[i + 1])
            mixed = mix(tops(now, bounded), values(s, slice(64 * t, 64 * t + 64)), lane % BLK, asked[s])
            mixes[at[s], 64 * t : 64 * t + HEAD, :BLK] = mixed[:HEAD, :BLK].astype(jnp.bfloat16)
            mixes[at[s], 64 * t + HEAD : 64 * t + 64, :BLK] = mixed[HEAD:, BLK:].astype(jnp.bfloat16)
        for s in halves:
            mixes[at[s], :, BLK:] = jnp.zeros((C, BLK), jnp.bfloat16)

        most = functools.reduce(jnp.maximum, asked.values())

        def more(b, carry):
            start = b * QB
            stacked = [rest_stacked(start, s) for s in halves]
            scores = [[dot_nn(key, x) for key in keys[s]] for s, x in zip(halves, stacked)]
            placed = [rest_mixed(start, s, score) for s, score in zip(halves, scores)]
            for s, x in zip(halves, placed):
                mixes[at[s], :, BLK:] = (mixes[at[s], :, BLK:].astype(jnp.float32) + x).astype(jnp.bfloat16)
            return carry

        def rest():
            none = jnp.zeros((HEAD, BLK), jnp.float32)
            stacked = []
            for s in halves:
                rows = []
                for h in range(HEADS):
                    x = qt[at[s], HEAD * h : HEAD * h + HEAD, BLK:].astype(jnp.float32)
                    x = jnp.where(iota((HEAD, BLK), 1) < QB, x, 0.0)
                    x = pltpu.roll(x, QB * (h % 4), 1) if h % 4 else x
                    rows.append(jnp.concatenate([x, none] if h < 4 else [none, x], axis=1))
                stacked.append(jnp.concatenate(rows, axis=0).astype(jnp.bfloat16))
            scores = [[dot_nn(key, x) for key in keys[s]] for s, x in zip(halves, stacked)]
            mixed = [
                mix(tops(score, bounded), values(s, slice(0, C)), BLK + lane % QB, asked[s]) for s, score in zip(halves, scores)
            ]
            for s, x in zip(halves, mixed):
                for h in range(HEADS):
                    piece = x[HEAD * h : HEAD * h + HEAD, BLK * (h // 4) : BLK * (h // 4) + BLK]
                    piece = pltpu.roll(piece, BLK - QB * (h % 4), 1) if h % 4 else piece
                    piece = jnp.where(iota((HEAD, BLK), 1) < QB, piece, 0.0)
                    mixes[at[s], HEAD * h : HEAD * h + HEAD, BLK:] = piece.astype(jnp.bfloat16)

        pl.when((most > BLK) & (most <= BLK + QB))(rest)
        if size > BLK + QB:
            blocks = (most + QB - 1) // QB
            lax.fori_loop(jnp.where(most > BLK + QB, BLK // QB, blocks), blocks, more, 0)

    def window(w, carry):
        at = 2 * w
        largest = jnp.maximum(jnp.maximum(counts[at], counts[at + 1]), jnp.maximum(count_far[2 * w], count_far[2 * w + 1]))
        active = jnp.maximum(counts[2 * n + at], counts[2 * n + at + 1]) > 0

        @pl.when(jnp.logical_not(active))
        def _():
            for s in range(2):
                mixes[2 * w + s] = jnp.zeros_like(mixes[2 * w + s])

        under = -1
        for size in SIZES:
            pl.when(active & safe & (largest > under) & (largest <= size))(functools.partial(attend, w, {0: 0, 1: 1}, size, True))
            under = size

        @pl.when(active & jnp.logical_not(safe & (largest <= under)))
        def _():
            def general(s, carry):
                attend(w, {0: s}, HALF, False)
                return carry

            lax.fori_loop(0, 2, general, 0)

        return carry

    lax.fori_loop(0, n, window, 0)

    for i in range(0, 2 * n, 4):
        items = [(j // 2, j % 2) for j in range(i, min(i + 4, 2 * n))]
        delta_t = [dot_nn(woutt[...], mixes[2 * w + s]).astype(jnp.bfloat16) for w, s in items]
        delta = [dot_nt(spread[2 * w + s], x) for (w, s), x in zip(items, delta_t)]
        for (w, s), x in zip(items, delta):
            if s == 1:
                x = jnp.where(flags[0] == 1, 0.0, x)
            out[w, s] = x.astype(jnp.bfloat16).reshape(2, BLK, C)


def far_half(edges, flags, near, far_a, far_b, gain, w_qkv, w_out):
    k_near, vt_near, qt, spread, counts, peaks = near
    n = counts.shape[0] // 4
    return pl.pallas_call(
        functools.partial(far_kernel, n),
        out_shape=jax.ShapeDtypeStruct((n, 2, 2, BLK, C), jnp.bfloat16),
        in_specs=[SMEM] * 3 + [VMEM] * 9,
        out_specs=VMEM,
        scratch_shapes=[
            pltpu.VMEM((16, C), jnp.float32),
            pltpu.VMEM((2 * n, HALF, C), jnp.bfloat16),
            pltpu.VMEM((2 * n, C + ONES, HALF), jnp.bfloat16),
            pltpu.VMEM((C, C), jnp.bfloat16),
            pltpu.VMEM((C, C), jnp.bfloat16),
            pltpu.VMEM((8, BLK), jnp.float32),
            pltpu.VMEM((2 * n, C, HALF), jnp.bfloat16),
            pltpu.SMEM((2 * n,), jnp.int32),
        ],
        compiler_params=PARAMS,
        cost_estimate=pl.CostEstimate(flops=n * 10**9, bytes_accessed=n * 10**6, transcendentals=0),
        name="windows_edge" if edges else "windows_inner",
    )(flags, counts, peaks, far_a, far_b, gain, w_qkv, w_out, k_near, vt_near, qt, spread)


def permute(x, pairs):
    return lax.ppermute(x, ("lon", "lat"), pairs)


def shards(state, ocean_mask, norm_gain, w_qkv, w_out):
    lon_n, lat_n = lax.axis_size("lon"), lax.axis_size("lat")
    lat = lax.axis_index("lat")
    at = lambda i, j: i * lat_n + j
    every = [(i, j) for i in range(lon_n) for j in range(lat_n)]
    go_a = [(at(i, j), at(i, j - 1 if j % 2 else j + 1)) for i, j in every]
    go_b = [(at(i, j), at(i, j + 1 if j % 2 else j - 1)) for i, j in every if 0 < j < lat_n - 1]
    go_b += [(at(i, lat_n - 1), at(lon_n - 1 - i, lat_n - 1)) for i in range(lon_n)]
    go_east = [(at(i, j), at((i + 1) % lon_n, j)) for i, j in every]
    go_west = [(at(i, j), at((i - 1) % lon_n, j)) for i, j in every]

    flags = jnp.stack([lat == 0, lat == lat_n - 1, lat % 2 == 1]).astype(jnp.int32)
    inner_a, inner_b, outer_a, outer_b, to_east, to_west = prep(flags, state, ocean_mask, RIM)
    west = permute(to_east, go_east)
    east = permute(to_west, go_west)
    far_a = permute(inner_a, go_a)
    far_b = permute(inner_b, go_b)
    rim = lambda x, s: jnp.concatenate([x[:1], west[s : s + 1], x[1:], east[s : s + 1]])
    outer_a, outer_b = rim(outer_a, 0), rim(outer_b, 1)
    rim_a = permute(outer_a, go_a)
    rim_b = permute(outer_b, go_b)

    gain = norm_gain[None, :]
    inner_a, inner_b, outer_a, outer_b = lax.optimization_barrier((inner_a, inner_b, outer_a, outer_b))
    near = near_half(False, inner_a, inner_b, gain, w_qkv)
    near_rim = near_half(True, outer_a, outer_b, gain, w_qkv)
    near, near_rim = lax.optimization_barrier((near, near_rim))
    inner = far_half(False, flags, near, far_a, far_b, gain, w_qkv, w_out)
    inner, near_rim = lax.optimization_barrier((inner, near_rim))
    outer = far_half(True, flags, near_rim, rim_a, rim_b, gain, w_qkv, w_out)
    return finish(flags, state, inner, outer)


def solution(mesh):
    in_specs = (P(None, "lat", "lon", None), P(None, "lat", "lon"), P(), P(), P())
    out_specs = P(None, "lat", "lon", None)
    return jax.shard_map(shards, mesh=mesh, in_specs=in_specs, out_specs=out_specs, check_vma=False)
```

```python
import functools

import jax
import jax.numpy as jnp
from jax import lax
from jax.experimental import pallas as pl
from jax.experimental.pallas import tpu as pltpu
from jax.sharding import PartitionSpec as P

C = 256
HEADS = 8
HEAD = C // HEADS
W = 16
SHIFT = 8
LEV = 2
HALF = W * W * LEV // 2
BLK = HALF // 2
QB = 32
ONES = 16
SIZES = (144, 176)
GROUP = 4
RIM = 3
LAND = 1024.0
SAFE_SQ = 60.0**2
SAFE_WEIGHT = 1e6

VMEM = pl.BlockSpec(memory_space=pltpu.VMEM)
SMEM = pl.BlockSpec(memory_space=pltpu.SMEM)
ANY = pl.BlockSpec(memory_space=pl.ANY)
PARAMS = pltpu.CompilerParams(vmem_limit_bytes=36 * 1024 * 1024)


def dot_nt(a, b):
    return lax.dot_general(a, b, (((1,), (1,)), ((), ())), preferred_element_type=jnp.float32)


def dot_nn(a, b):
    return jnp.dot(a, b, preferred_element_type=jnp.float32)


def iota(shape, axis):
    return lax.broadcasted_iota(jnp.int32, shape, axis)


def one(condition):
    return jnp.where(condition, 1.0, 0.0).astype(jnp.bfloat16)


def ocean_ranks(halves, rows_n):
    channel, row = iota((rows_n, C), 1), iota((rows_n, C), 0)
    marks = None
    for i, half in enumerate(halves):
        part = dot_nt(one((channel == 0) & (row == i)), half)
        marks = part if marks is None else marks + part
    ocean = jnp.where(marks < LAND / 2, 1.0, 0.0)
    return dot_nn(ocean.astype(jnp.bfloat16), one(iota((C, C), 0) <= iota((C, C), 1))) * ocean


def packed_norm(tokens, ranks, count, size, gain):
    wanted = jnp.minimum(iota((size, 1), 0) + 1, count).astype(jnp.float32)
    packed = dot_nn(one(ranks == wanted), tokens)
    average = jnp.mean(packed, axis=1, keepdims=True)
    centred = packed - average
    spread_sq = jnp.mean(centred * centred, axis=1, keepdims=True)
    return (centred * lax.rsqrt(spread_sq + 1e-05) * gain).astype(jnp.bfloat16)


def valid_rows(x, count):
    return jnp.where(iota((x.shape[0], 1), 0) < count, x.astype(jnp.float32), 0.0).astype(jnp.bfloat16)


def valid_ones(count, size):
    return one(jnp.broadcast_to(iota((1, size), 1) < count, (ONES, size)))


def head_norms(keys, sums):
    return jnp.max(dot_nn((keys * keys).astype(jnp.bfloat16), sums), axis=0, keepdims=True)


def fill(keys, values, i, key, size):
    keys[i, size:, :] = jnp.broadcast_to(key[0:1].astype(jnp.float32), (HALF - size, C)).astype(jnp.bfloat16)
    values[i, :, size:] = jnp.zeros((C + ONES, HALF - size), jnp.bfloat16)


def prep_kernel(flags, state, mask, inner_a, inner_b, outer_a, outer_b, to_east, to_west):
    blocks = state.shape[2] // SHIFT
    cols = blocks * SHIFT
    rim = outer_a.shape[0] // 2
    eye = one(iota((cols, cols), 0) == iota((cols, cols), 1))
    by_column = [dot_nt(eye, mask[level]).astype(jnp.bfloat16) for level in range(LEV)]
    for s, inner, outer in ((0, inner_a, outer_a), (1, inner_b, outer_b)):
        first = jnp.where(flags[2] == s, SHIFT, 0)
        for level in range(LEV):
            for p in range(SHIFT // 2):
                pair = []
                for row in (2 * p, 2 * p + 1):
                    chosen = one(iota((2 * SHIFT, BLK), 0) == first + row)
                    ocean = dot_nn(by_column[level], chosen)
                    ocean = jnp.concatenate([ocean, ocean], axis=1)
                    values = state[level, first + row].astype(jnp.float32)
                    pair.append(jnp.where(ocean > 0.5, values, LAND).reshape(blocks, SHIFT, C))
                both = jnp.concatenate(pair, axis=1).astype(jnp.bfloat16)
                at = pl.ds((BLK // 2) * level + 2 * SHIFT * p, 2 * SHIFT)
                inner[:, at, :] = both[rim : blocks - rim]
                outer[:rim, at, :] = both[:rim]
                outer[rim:, at, :] = both[blocks - rim :]
                to_east[s, at, :] = both[blocks - 1]
                to_west[s, at, :] = both[0]


def prep(flags, state, mask, rim):
    blocks = state.shape[2] // SHIFT
    shape = lambda n: jax.ShapeDtypeStruct((n, BLK, C), jnp.bfloat16)
    return pl.pallas_call(
        prep_kernel,
        out_shape=(shape(blocks - 2 * rim),) * 2 + (shape(2 * rim),) * 2 + (shape(2),) * 2,
        in_specs=[SMEM, VMEM, VMEM],
        out_specs=(VMEM,) * 6,
        compiler_params=PARAMS,
        name="windows_prep",
    )(flags, state, mask.astype(jnp.bfloat16))


def finish(flags, state, inner, outer, sums, out, sems):
    blocks = state.shape[2] // SHIFT
    rim = (blocks - 2 * inner.shape[0]) // 2
    half = SHIFT // 2
    copies = []
    for level in range(LEV):
        for quarter in range(state.shape[1] // half):
            s = flags[2] if quarter // 2 == 1 else 1 - flags[2]
            for p in range(half // 2):
                at = pl.ds(level * (BLK // 2) + SHIFT * (half * (quarter % 2) + 2 * p), 2 * SHIFT)
                deltas = []
                for b in range(blocks):
                    if b < rim:
                        delta = outer[(b + 1) // 2, s, 0 if b == 0 else 1 - b % 2, at, :]
                    elif b < blocks - rim:
                        delta = inner[(b - rim) // 2, s, (b - rim) % 2, at, :]
                    else:
                        k = b - (blocks - rim)
                        delta = outer[(rim + 1) // 2 + k // 2, s, k % 2, at, :]
                    deltas.append(delta.astype(jnp.float32))
                for i in range(2):
                    added = jnp.concatenate([d[SHIFT * i : SHIFT * i + SHIFT] for d in deltas], axis=0)
                    row = half * quarter + 2 * p + i
                    sums[level, row] = (state[level, row].astype(jnp.float32) + added).astype(jnp.bfloat16)
            rows = pl.ds(half * quarter, half)
            copies.append(pltpu.make_async_copy(sums.at[level, rows], out.at[level, rows], sems.at[len(copies)]))
            copies[-1].start()
    for copy in copies:
        copy.wait()


def for_halves(spans, counts, work):
    largest = functools.reduce(jnp.maximum, [counts[i] for i in range(2 * spans[0][0], 2 * spans[-1][1])])
    size = SIZES[-1]

    @pl.when(largest <= size)
    def _():
        for i, (start, end) in enumerate(spans):
            items = [(w, s) for w in range(start, end) for s in range(2)]
            for at in range(0, len(items), GROUP):
                work(size, items[at : at + GROUP], i)

    @pl.when(largest > size)
    def _():
        for i, (start, end) in enumerate(spans):

            def step(w, carry, i=i):
                work(HALF, [(w, 0), (w, 1)], i)
                return carry

            lax.fori_loop(start, end, step, 0)


def near_kernel(spans, inner_a, inner_b, outer_a, outer_b, gain, w_qkv, k_out, vt_out, qt_out, spread_out, counts, peaks, ranks, wqt, wvt, norms):
    parts = ((inner_a, inner_b), (outer_a, outer_b))
    n = spans[-1][1]

    def tokens_at(w, s, span):
        return parts[span][s][pl.ds(2 * (w - spans[span][0]), 2)].reshape(HALF, C)

    halves = [(w, s, i) for i, (start, end) in enumerate(spans) for w in range(start, end) for s in range(2)]
    rank = ocean_ranks([tokens_at(*half) for half in halves], 32)
    ranks[...] = rank
    for i in range(2 * n):
        counts[i] = jnp.max(rank[i : i + 1, :]).astype(jnp.int32)
        is_edge = i // 2 in (spans[1][0], n - 1)
        counts[2 * n + i] = jnp.max(rank[i : i + 1, :BLK]).astype(jnp.int32) if is_edge else counts[i]

    eye = one(iota((C, C), 0) == iota((C, C), 1))
    wqt[...] = dot_nt(eye, w_qkv[:, :C]).astype(jnp.bfloat16)
    wvt[...] = dot_nt(eye, w_qkv[:, 2 * C :]).astype(jnp.bfloat16)
    norms[...] = jnp.zeros_like(norms)
    by_column = dot_nt(eye, rank.astype(jnp.bfloat16)).astype(jnp.bfloat16)
    for i in range(2 * n):
        col_rank = dot_nn(by_column, one(iota((32, BLK), 0) == i))
        for at in (0, BLK):
            number = (iota((HALF, BLK), 1) + (at + 1)).astype(jnp.float32)
            spread_out[i, :, at : at + BLK] = one(col_rank == number)

    def window(size, items, span):
        sums = one(iota((C, BLK), 0) // HEAD == iota((C, BLK), 1))
        sums_t = one(iota((ONES, C), 1) // HEAD == iota((ONES, C), 0))
        count = [counts[2 * w + s] for w, s in items]
        normed = [
            packed_norm(tokens_at(w, s, span), ranks[pl.ds(2 * w + s, 1), :], c, size, gain[...]) for (w, s), c in zip(items, count)
        ]
        keys = [dot_nn(x, w_qkv[:, C : 2 * C]).astype(jnp.bfloat16) for x in normed]
        queries = [(dot_nt(wqt[...], x) * (1.0 / HEAD**0.5)).astype(jnp.bfloat16) for x in normed]
        values = [dot_nt(wvt[...], valid_rows(x, c)).astype(jnp.bfloat16) for x, c in zip(normed, count)]
        for (w, s), c, key, query, value in zip(items, count, keys, queries, values):
            k_out[2 * w + s, :size, :] = key
            qt_out[2 * w + s, :, :size] = query
            vt_out[2 * w + s, :C, :size] = value
            vt_out[2 * w + s, C:, :size] = valid_ones(c, size)
            if size < HALF:
                qt_out[2 * w + s, :, size:] = jnp.zeros((C, HALF - size), jnp.bfloat16)
                fill(k_out, vt_out, 2 * w + s, key, size)
            norms[0:1, :] = jnp.maximum(norms[0:1, :], head_norms(key, sums))
            by_head = dot_nn(sums_t, query * query)
            norms[8:, :] = jnp.maximum(norms[8:, :], jnp.max(by_head, axis=1, keepdims=True))

    for_halves(spans, counts, window)
    peaks[0] = jnp.max(norms[0:1, :])
    peaks[1] = jnp.max(norms[8:, :])


def near_half(inner_a, inner_b, outer_a, outer_b, gain, w_qkv):
    middle = inner_a.shape[0] // 2
    n = middle + outer_a.shape[0] // 2
    bf = lambda *shape: jax.ShapeDtypeStruct(shape, jnp.bfloat16)
    return pl.pallas_call(
        functools.partial(near_kernel, ((0, middle), (middle, n))),
        out_shape=(
            bf(2 * n, HALF, C),
            bf(2 * n, C + ONES, HALF),
            bf(2 * n, C, HALF),
            bf(2 * n, HALF, HALF),
            jax.ShapeDtypeStruct((4 * n,), jnp.int32),
            jax.ShapeDtypeStruct((2,), jnp.float32),
        ),
        in_specs=[VMEM] * 6,
        out_specs=(VMEM,) * 4 + (SMEM,) * 2,
        scratch_shapes=[
            pltpu.VMEM((32, C), jnp.float32),
            pltpu.VMEM((C, C), jnp.bfloat16),
            pltpu.VMEM((C, C), jnp.bfloat16),
            pltpu.VMEM((8 + ONES, BLK), jnp.float32),
        ],
        compiler_params=PARAMS,
        cost_estimate=pl.CostEstimate(flops=n * 10**9, bytes_accessed=n * 10**6, transcendentals=0),
        name="windows_near",
    )(inner_a, inner_b, outer_a, outer_b, gain, w_qkv)


def tops(scores, bounded):
    if bounded:
        return scores
    top = jnp.maximum(jnp.max(scores[0], axis=0, keepdims=True), jnp.max(scores[1], axis=0, keepdims=True))
    return [score - top for score in scores]


def mix(scores, values, slots, queries_n):
    parts = [dot_nn(value, jnp.exp(score).astype(jnp.bfloat16)) for score, value in zip(scores, values)]
    summed = parts[0] + parts[1]
    n = summed.shape[0] - ONES
    total = summed[n : n + 1, :] + jnp.where(slots < queries_n, 0.0, 1.0)
    return summed[:n, :] * (1.0 / total)


def far_kernel(first, n, flags, counts, peaks, far_a, far_b, gain, w_qkv, w_out, k_near, vt_near, qt, spread, *refs):
    if len(refs) > 9:
        state, inner, result, ranks, k_far, vt_far, wvt, woutt, norms, mixes, count_far, out, sums, sems = refs
    else:
        out, ranks, k_far, vt_far, wvt, woutt, norms, mixes, count_far = refs
    far_refs = (far_a, far_b)

    def tokens_at(w, s):
        i = jnp.where(flags[1] == 1, n - 1 - w, w) if s == 1 else w
        return far_refs[s][pl.ds(2 * i, 2)].reshape(HALF, C)

    rank = ocean_ranks([tokens_at(i // 2, i % 2) for i in range(2 * n)], 16)
    ranks[...] = rank
    for i in range(2 * n):
        found = jnp.max(rank[i : i + 1, :]).astype(jnp.int32)
        count_far[i] = jnp.where(flags[0] == 1, 0, found) if i % 2 else found
    eye = one(iota((C, C), 0) == iota((C, C), 1))
    wvt[...] = dot_nt(eye, w_qkv[:, 2 * C :]).astype(jnp.bfloat16)
    woutt[...] = dot_nt(eye, w_out[...]).astype(jnp.bfloat16)
    norms[...] = jnp.zeros_like(norms)

    def prepare(size, items, span):
        sums = one(iota((C, BLK), 0) // HEAD == iota((C, BLK), 1))
        count = [count_far[2 * w + s] for w, s in items]
        normed = [
            packed_norm(tokens_at(w, s), ranks[pl.ds(2 * w + s, 1), :], c, size, gain[...]) for (w, s), c in zip(items, count)
        ]
        keys = [dot_nn(x, w_qkv[:, C : 2 * C]).astype(jnp.bfloat16) for x in normed]
        values = [dot_nt(wvt[...], valid_rows(x, c)).astype(jnp.bfloat16) for x, c in zip(normed, count)]
        for (w, s), c, key, value in zip(items, count, keys, values):
            k_far[2 * w + s, :size, :] = key
            vt_far[2 * w + s, :C, :size] = value
            vt_far[2 * w + s, C:, :size] = valid_ones(c, size)
            if size < HALF:
                fill(k_far, vt_far, 2 * w + s, key, size)
            norms[0:1, :] = jnp.maximum(norms[0:1, :], head_norms(key, sums))

    for_halves(((0, n),), count_far, prepare)
    peak = jnp.maximum(jnp.max(norms[0:1, :]), peaks[0]) * peaks[1]
    largest_weight = jnp.max(jnp.abs(w_qkv[:, 2 * C :].astype(jnp.float32)))
    asked_from = counts.shape[0] // 2
    safe = (peak <= SAFE_SQ) & (largest_weight <= SAFE_WEIGHT)

    lane = iota((1, C), 1)

    def attend(w, halves, size, bounded, fused):
        at = {k: 2 * w + s for k, s in halves.items()}
        near_at = {k: 2 * first + i for k, i in at.items()}
        asked = {k: counts[asked_from + i] for k, i in near_at.items()}
        keys = {s: [k_near[near_at[s], :size, :], k_far[at[s], :size, :]] for s in halves}
        if not bounded:
            for s in halves:
                near, far = [key.astype(jnp.float32) for key in keys[s]]
                far = jnp.where(count_far[at[s]] > 0, far, jnp.broadcast_to(near[0:1], far.shape))
                keys[s][1] = far.astype(jnp.bfloat16)

        def values(s, rows):
            return [
                jnp.concatenate([ref[i, rows, :size], ref[i, C : C + ONES, :size]], axis=0)
                for ref, i in ((vt_near, near_at[s]), (vt_far, at[s]))
            ]

        def base_scores(t, s):
            g = t // 2
            none = jnp.zeros((HEAD, BLK), jnp.bfloat16)
            rows = []
            for h in range(4 * g, 4 * g + 4):
                mine = qt[near_at[s], HEAD * h : HEAD * h + HEAD, :BLK] if h // 2 == t else none
                rows.append(jnp.concatenate([mine, none] if h % 2 == 0 else [none, mine], axis=1))
            stacked = jnp.concatenate(rows, axis=0)
            return [dot_nn(key[:, BLK * g : BLK * g + BLK], stacked) for key in keys[s]]

        sub, lan = iota((C, C), 0), iota((C, C), 1)
        block = sub // HEAD == lan // QB

        def rest_stacked(start, s):
            repeat = one(sub[:BLK] + BLK == start + lan[:BLK] % QB)
            return jnp.where(block, dot_nn(qt[near_at[s], :, BLK:], repeat), 0.0).astype(jnp.bfloat16)

        def rest_mixed(start, s, scores):
            mixed = mix(tops(scores, bounded), values(s, slice(0, C)), start + lane % QB, asked[s])
            mixed = jnp.where(block, mixed, 0.0).astype(jnp.bfloat16)
            return dot_nn(mixed, one(sub[:, :BLK] % QB + start == lan[:, :BLK] + BLK))

        def rolled(s):
            none = jnp.zeros((HEAD, BLK), jnp.float32)
            rows = []
            for h in range(HEADS):
                x = qt[near_at[s], HEAD * h : HEAD * h + HEAD, BLK:].astype(jnp.float32)
                x = jnp.where(iota((HEAD, BLK), 1) < QB, x, 0.0)
                x = pltpu.roll(x, QB * (h % 4), 1) if h % 4 else x
                rows.append(jnp.concatenate([x, none] if h < 4 else [none, x], axis=1))
            return jnp.concatenate(rows, axis=0).astype(jnp.bfloat16)

        def unroll(s, mixed):
            for h in range(HEADS):
                piece = mixed[HEAD * h : HEAD * h + HEAD, BLK * (h // 4) : BLK * (h // 4) + BLK]
                piece = pltpu.roll(piece, BLK - QB * (h % 4), 1) if h % 4 else piece
                piece = jnp.where(iota((HEAD, BLK), 1) < QB, piece, 0.0)
                mixes[at[s], HEAD * h : HEAD * h + HEAD, BLK:] = piece.astype(jnp.bfloat16)

        tiles = [(t, s) for t in range(4) for s in halves]
        if fused:
            stacked = {s: rolled(s) for s in halves}
            tiles = tiles[:2] + [(4, s) for s in halves] + tiles[2:]

        def tile_scores(t, s):
            return [dot_nn(key, stacked[s]) for key in keys[s]] if t == 4 else base_scores(t, s)

        ahead = tile_scores(*tiles[0])
        for i, (t, s) in enumerate(tiles):
            now = ahead
            if i + 1 < len(tiles):
                ahead = tile_scores(*tiles[i + 1])
            if t == 4:
                unroll(s, mix(tops(now, bounded), values(s, slice(0, C)), BLK + lane % QB, asked[s]))
                continue
            mixed = mix(tops(now, bounded), values(s, slice(64 * t, 64 * t + 64)), lane % BLK, asked[s])
            mixes[at[s], 64 * t : 64 * t + HEAD, :BLK] = mixed[:HEAD, :BLK].astype(jnp.bfloat16)
            mixes[at[s], 64 * t + HEAD : 64 * t + 64, :BLK] = mixed[HEAD:, BLK:].astype(jnp.bfloat16)
        if fused:
            return
        for s in halves:
            mixes[at[s], :, BLK:] = jnp.zeros((C, BLK), jnp.bfloat16)
        if bounded:
            return

        most = functools.reduce(jnp.maximum, asked.values())

        def more(b, carry):
            start = b * QB
            stacked = [rest_stacked(start, s) for s in halves]
            scores = [[dot_nn(key, x) for key in keys[s]] for s, x in zip(halves, stacked)]
            placed = [rest_mixed(start, s, score) for s, score in zip(halves, scores)]
            for s, x in zip(halves, placed):
                mixes[at[s], :, BLK:] = (mixes[at[s], :, BLK:].astype(jnp.float32) + x).astype(jnp.bfloat16)
            return carry

        lax.fori_loop(BLK // QB, (most + QB - 1) // QB, more, 0)

    def window(w, carry):
        at = 2 * first + 2 * w
        largest = jnp.maximum(jnp.maximum(counts[at], counts[at + 1]), jnp.maximum(count_far[2 * w], count_far[2 * w + 1]))
        most = jnp.maximum(counts[asked_from + at], counts[asked_from + at + 1])
        active = most > 0
        easy = safe & (largest <= SIZES[-1]) & (most <= BLK + QB)

        @pl.when(jnp.logical_not(active))
        def _():
            for s in range(2):
                mixes[2 * w + s] = jnp.zeros_like(mixes[2 * w + s])

        under = -1
        for size in SIZES:
            fits = active & easy & (largest > under) & (largest <= size)
            pl.when(fits & (most <= BLK))(functools.partial(attend, w, {0: 0, 1: 1}, size, True, False))
            pl.when(fits & (most > BLK))(functools.partial(attend, w, {0: 0, 1: 1}, size, True, True))
            under = size

        @pl.when(active & jnp.logical_not(easy))
        def _():
            def general(s, carry):
                attend(w, {0: s}, HALF, False, False)
                return carry

            lax.fori_loop(0, 2, general, 0)

        return carry

    lax.fori_loop(0, n, window, 0)

    for i in range(0, 2 * n, 4):
        items = [(j // 2, j % 2) for j in range(i, min(i + 4, 2 * n))]
        delta_t = [dot_nn(woutt[...], mixes[2 * w + s]).astype(jnp.bfloat16) for w, s in items]
        delta = [dot_nt(spread[2 * first + 2 * w + s], x) for (w, s), x in zip(items, delta_t)]
        for (w, s), x in zip(items, delta):
            if s == 1:
                x = jnp.where(flags[0] == 1, 0.0, x)
            out[w, s] = x.astype(jnp.bfloat16).reshape(2, BLK, C)

    if len(refs) > 9:
        finish(flags, state, inner, out, sums, result, sems)


def far_half(flags, near, far_a, far_b, gain, w_qkv, w_out, state=None, inner=None):
    k_near, vt_near, qt, spread, counts, peaks = near
    n = far_a.shape[0] // 2
    last = state is not None
    first = counts.shape[0] // 4 - n if last else 0
    deltas = (n, 2, 2, BLK, C)
    scratch = [
        pltpu.VMEM((16, C), jnp.float32),
        pltpu.VMEM((2 * n, HALF, C), jnp.bfloat16),
        pltpu.VMEM((2 * n, C + ONES, HALF), jnp.bfloat16),
        pltpu.VMEM((C, C), jnp.bfloat16),
        pltpu.VMEM((C, C), jnp.bfloat16),
        pltpu.VMEM((8, BLK), jnp.float32),
        pltpu.VMEM((2 * n, C, HALF), jnp.bfloat16),
        pltpu.SMEM((2 * n,), jnp.int32),
    ]
    if last:
        scratch += [pltpu.VMEM(deltas, jnp.bfloat16), pltpu.VMEM(state.shape, state.dtype), pltpu.SemaphoreType.DMA((8,))]
    return pl.pallas_call(
        functools.partial(far_kernel, first, n),
        out_shape=jax.ShapeDtypeStruct(state.shape if last else deltas, jnp.bfloat16),
        in_specs=[SMEM] * 3 + [VMEM] * (11 if last else 9),
        out_specs=ANY if last else VMEM,
        scratch_shapes=scratch,
        compiler_params=PARAMS,
        cost_estimate=pl.CostEstimate(flops=n * 10**9, bytes_accessed=n * 10**6, transcendentals=0),
        name="windows_edge" if last else "windows_inner",
    )(flags, counts, peaks, far_a, far_b, gain, w_qkv, w_out, k_near, vt_near, qt, spread, *((state, inner) if last else ()))


def permute(x, pairs):
    return lax.ppermute(x, ("lon", "lat"), pairs)


def shards(state, ocean_mask, norm_gain, w_qkv, w_out):
    lon_n, lat_n = lax.axis_size("lon"), lax.axis_size("lat")
    lat = lax.axis_index("lat")
    at = lambda i, j: i * lat_n + j
    every = [(i, j) for i in range(lon_n) for j in range(lat_n)]
    go_a = [(at(i, j), at(i, j - 1 if j % 2 else j + 1)) for i, j in every]
    go_b = [(at(i, j), at(i, j + 1 if j % 2 else j - 1)) for i, j in every if 0 < j < lat_n - 1]
    go_b += [(at(i, lat_n - 1), at(lon_n - 1 - i, lat_n - 1)) for i in range(lon_n)]
    go_east = [(at(i, j), at((i + 1) % lon_n, j)) for i, j in every]
    go_west = [(at(i, j), at((i - 1) % lon_n, j)) for i, j in every]

    flags = jnp.stack([lat == 0, lat == lat_n - 1, lat % 2 == 1]).astype(jnp.int32)
    inner_a, inner_b, outer_a, outer_b, to_east, to_west = prep(flags, state, ocean_mask, RIM)
    west = permute(to_east, go_east)
    east = permute(to_west, go_west)
    far_a = permute(inner_a, go_a)
    far_b = permute(inner_b, go_b)
    rim = lambda x, s: jnp.concatenate([x[:1], west[s : s + 1], x[1:], east[s : s + 1]])
    outer_a, outer_b = rim(outer_a, 0), rim(outer_b, 1)
    rim_a = permute(outer_a, go_a)
    rim_b = permute(outer_b, go_b)

    gain = norm_gain[None, :]
    inner_a, inner_b, outer_a, outer_b = lax.optimization_barrier((inner_a, inner_b, outer_a, outer_b))
    near = near_half(inner_a, inner_b, outer_a, outer_b, gain, w_qkv)
    inner = far_half(flags, near, far_a, far_b, gain, w_qkv, w_out)
    return far_half(flags, near, rim_a, rim_b, gain, w_qkv, w_out, state, inner)


def solution(mesh):
    in_specs = (P(None, "lat", "lon", None), P(None, "lat", "lon"), P(), P(), P())
    out_specs = P(None, "lat", "lon", None)
    return jax.shard_map(shards, mesh=mesh, in_specs=in_specs, out_specs=out_specs, check_vma=False)
```

```python
import functools

import jax
import jax.numpy as jnp
from jax import lax
from jax.experimental import pallas as pl
from jax.experimental.pallas import tpu as pltpu
from jax.sharding import PartitionSpec as P

C = 256
HEADS = 8
HEAD = C // HEADS
W = 16
SHIFT = 8
LEV = 2
HALF = W * W * LEV // 2
BLK = HALF // 2
QB = 32
ONES = 16
SIZES = (144, 176)
GROUP = 10
RIM = 3
LAND = 1024.0
SAFE_SQ = 60.0**2
SAFE_WEIGHT = 1e6

VMEM = pl.BlockSpec(memory_space=pltpu.VMEM)
SMEM = pl.BlockSpec(memory_space=pltpu.SMEM)
ANY = pl.BlockSpec(memory_space=pl.ANY)
PARAMS = pltpu.CompilerParams(vmem_limit_bytes=36 * 1024 * 1024)


def dot_nt(a, b):
    return lax.dot_general(a, b, (((1,), (1,)), ((), ())), preferred_element_type=jnp.float32)


def dot_nn(a, b):
    return jnp.dot(a, b, preferred_element_type=jnp.float32)


def iota(shape, axis):
    return lax.broadcasted_iota(jnp.int32, shape, axis)


def one(condition):
    return jnp.where(condition, 1.0, 0.0).astype(jnp.bfloat16)


def ocean_ranks(halves, rows_n):
    channel, row = iota((rows_n, C), 1), iota((rows_n, C), 0)
    marks = None
    for i, half in enumerate(halves):
        part = dot_nt(one((channel == 0) & (row == i)), half)
        marks = part if marks is None else marks + part
    ocean = jnp.where(marks < LAND / 2, 1.0, 0.0)
    return dot_nn(ocean.astype(jnp.bfloat16), one(iota((C, C), 0) <= iota((C, C), 1))) * ocean


def packed_norm(tokens, ranks, count, size, gain):
    wanted = jnp.minimum(iota((size, 1), 0) + 1, count).astype(jnp.float32)
    packed = dot_nn(one(ranks == wanted), tokens)
    average = jnp.mean(packed, axis=1, keepdims=True)
    centred = packed - average
    spread_sq = jnp.mean(centred * centred, axis=1, keepdims=True)
    return (centred * lax.rsqrt(spread_sq + 1e-05) * gain).astype(jnp.bfloat16)


def valid_rows(x, count):
    return jnp.where(iota((x.shape[0], 1), 0) < count, x.astype(jnp.float32), 0.0).astype(jnp.bfloat16)


def valid_ones(count, size):
    return one(jnp.broadcast_to(iota((1, size), 1) < count, (ONES, size)))


def head_norms(keys, sums):
    return jnp.max(dot_nn((keys * keys).astype(jnp.bfloat16), sums), axis=0, keepdims=True)


def fill(keys, values, i, key, size):
    keys[i, size:, :] = jnp.broadcast_to(key[0:1].astype(jnp.float32), (HALF - size, C)).astype(jnp.bfloat16)
    values[i, :, size:] = jnp.zeros((C + ONES, HALF - size), jnp.bfloat16)


def prep_kernel(flags, state, mask, inner_a, inner_b, outer_a, outer_b, to_east, to_west):
    blocks = state.shape[2] // SHIFT
    cols = blocks * SHIFT
    rim = outer_a.shape[0] // 2
    eye = one(iota((cols, cols), 0) == iota((cols, cols), 1))
    by_column = [dot_nt(eye, mask[level]).astype(jnp.bfloat16) for level in range(LEV)]
    for s, inner, outer in ((0, inner_a, outer_a), (1, inner_b, outer_b)):
        first = jnp.where(flags[2] == s, SHIFT, 0)
        for level in range(LEV):
            for p in range(SHIFT // 2):
                pair = []
                for row in (2 * p, 2 * p + 1):
                    chosen = one(iota((2 * SHIFT, BLK), 0) == first + row)
                    ocean = dot_nn(by_column[level], chosen)
                    ocean = jnp.concatenate([ocean, ocean], axis=1)
                    values = state[level, first + row].astype(jnp.float32)
                    pair.append(jnp.where(ocean > 0.5, values, LAND).reshape(blocks, SHIFT, C))
                both = jnp.concatenate(pair, axis=1).astype(jnp.bfloat16)
                at = pl.ds((BLK // 2) * level + 2 * SHIFT * p, 2 * SHIFT)
                inner[:, at, :] = both[rim : blocks - rim]
                outer[:rim, at, :] = both[:rim]
                outer[rim:, at, :] = both[blocks - rim :]
                to_east[s, at, :] = both[blocks - 1]
                to_west[s, at, :] = both[0]


def prep(flags, state, mask, rim):
    blocks = state.shape[2] // SHIFT
    shape = lambda n: jax.ShapeDtypeStruct((n, BLK, C), jnp.bfloat16)
    return pl.pallas_call(
        prep_kernel,
        out_shape=(shape(blocks - 2 * rim),) * 2 + (shape(2 * rim),) * 2 + (shape(2),) * 2,
        in_specs=[SMEM, VMEM, VMEM],
        out_specs=(VMEM,) * 6,
        compiler_params=PARAMS,
        name="windows_prep",
    )(flags, state, mask.astype(jnp.bfloat16))


def finish(flags, state, inner, outer, sums, out, sems):
    blocks = state.shape[2] // SHIFT
    rim = (blocks - 2 * inner.shape[0]) // 2
    half = SHIFT // 2
    copies = []
    for level in range(LEV):
        for quarter in range(state.shape[1] // half):
            s = flags[2] if quarter // 2 == 1 else 1 - flags[2]
            for p in range(half // 2):
                at = pl.ds(level * (BLK // 2) + SHIFT * (half * (quarter % 2) + 2 * p), 2 * SHIFT)
                deltas = []
                for b in range(blocks):
                    if b < rim:
                        delta = outer[(b + 1) // 2, s, 0 if b == 0 else 1 - b % 2, at, :]
                    elif b < blocks - rim:
                        delta = inner[(b - rim) // 2, s, (b - rim) % 2, at, :]
                    else:
                        k = b - (blocks - rim)
                        delta = outer[(rim + 1) // 2 + k // 2, s, k % 2, at, :]
                    deltas.append(delta.astype(jnp.float32))
                for i in range(2):
                    added = jnp.concatenate([d[SHIFT * i : SHIFT * i + SHIFT] for d in deltas], axis=0)
                    row = half * quarter + 2 * p + i
                    sums[level, row] = (state[level, row].astype(jnp.float32) + added).astype(jnp.bfloat16)
            rows = pl.ds(half * quarter, half)
            copies.append(pltpu.make_async_copy(sums.at[level, rows], out.at[level, rows], sems.at[len(copies)]))
            copies[-1].start()
    for copy in copies:
        copy.wait()


def for_halves(spans, counts, work):
    largest = functools.reduce(jnp.maximum, [counts[i] for i in range(2 * spans[0][0], 2 * spans[-1][1])])
    size = SIZES[-1]

    @pl.when(largest <= size)
    def _():
        for i, (start, end) in enumerate(spans):
            items = [(w, s) for w in range(start, end) for s in range(2)]
            for at in range(0, len(items), GROUP):
                work(size, items[at : at + GROUP], i)

    @pl.when(largest > size)
    def _():
        for i, (start, end) in enumerate(spans):

            def step(w, carry, i=i):
                work(HALF, [(w, 0), (w, 1)], i)
                return carry

            lax.fori_loop(start, end, step, 0)


def near_kernel(spans, inner_a, inner_b, outer_a, outer_b, gain, w_qkv, k_out, vt_out, qt_out, spread_out, counts, peaks, ranks, wqt, wvt, norms):
    parts = ((inner_a, inner_b), (outer_a, outer_b))
    n = spans[-1][1]

    def tokens_at(w, s, span):
        return parts[span][s][pl.ds(2 * (w - spans[span][0]), 2)].reshape(HALF, C)

    halves = [(w, s, i) for i, (start, end) in enumerate(spans) for w in range(start, end) for s in range(2)]
    rank = ocean_ranks([tokens_at(*half) for half in halves], 32)
    ranks[...] = rank
    for i in range(2 * n):
        counts[i] = jnp.max(rank[i : i + 1, :]).astype(jnp.int32)
        is_edge = i // 2 in (spans[1][0], n - 1)
        counts[2 * n + i] = jnp.max(rank[i : i + 1, :BLK]).astype(jnp.int32) if is_edge else counts[i]

    eye = one(iota((C, C), 0) == iota((C, C), 1))
    wqt[...] = dot_nt(eye, w_qkv[:, :C]).astype(jnp.bfloat16)
    wvt[...] = dot_nt(eye, w_qkv[:, 2 * C :]).astype(jnp.bfloat16)
    norms[...] = jnp.zeros_like(norms)
    by_column = dot_nt(eye, rank.astype(jnp.bfloat16)).astype(jnp.bfloat16)
    for i in range(2 * n):
        col_rank = dot_nn(by_column, one(iota((32, BLK), 0) == i))
        for at in (0, BLK):
            number = (iota((HALF, BLK), 1) + (at + 1)).astype(jnp.float32)
            spread_out[i, :, at : at + BLK] = one(col_rank == number)

    def window(size, items, span):
        sums = one(iota((C, BLK), 0) // HEAD == iota((C, BLK), 1))
        sums_t = one(iota((ONES, C), 1) // HEAD == iota((ONES, C), 0))
        count = [counts[2 * w + s] for w, s in items]
        normed = [
            packed_norm(tokens_at(w, s, span), ranks[pl.ds(2 * w + s, 1), :], c, size, gain[...]) for (w, s), c in zip(items, count)
        ]
        keys = [dot_nn(x, w_qkv[:, C : 2 * C]).astype(jnp.bfloat16) for x in normed]
        queries = [(dot_nt(wqt[...], x) * (1.0 / HEAD**0.5)).astype(jnp.bfloat16) for x in normed]
        values = [dot_nt(wvt[...], valid_rows(x, c)).astype(jnp.bfloat16) for x, c in zip(normed, count)]
        for (w, s), c, key, query, value in zip(items, count, keys, queries, values):
            k_out[2 * w + s, :size, :] = key
            qt_out[2 * w + s, :, :size] = query
            vt_out[2 * w + s, :C, :size] = value
            vt_out[2 * w + s, C:, :size] = valid_ones(c, size)
            if size < HALF:
                qt_out[2 * w + s, :, size:] = jnp.zeros((C, HALF - size), jnp.bfloat16)
                fill(k_out, vt_out, 2 * w + s, key, size)
            norms[0:1, :] = jnp.maximum(norms[0:1, :], head_norms(key, sums))
            by_head = dot_nn(sums_t, query * query)
            norms[8:, :] = jnp.maximum(norms[8:, :], jnp.max(by_head, axis=1, keepdims=True))

    for_halves(spans, counts, window)
    peaks[0] = jnp.max(norms[0:1, :])
    peaks[1] = jnp.max(norms[8:, :])


def near_half(inner_a, inner_b, outer_a, outer_b, gain, w_qkv):
    middle = inner_a.shape[0] // 2
    n = middle + outer_a.shape[0] // 2
    bf = lambda *shape: jax.ShapeDtypeStruct(shape, jnp.bfloat16)
    return pl.pallas_call(
        functools.partial(near_kernel, ((0, middle), (middle, n))),
        out_shape=(
            bf(2 * n, HALF, C),
            bf(2 * n, C + ONES, HALF),
            bf(2 * n, C, HALF),
            bf(2 * n, HALF, HALF),
            jax.ShapeDtypeStruct((4 * n,), jnp.int32),
            jax.ShapeDtypeStruct((2,), jnp.float32),
        ),
        in_specs=[VMEM] * 6,
        out_specs=(VMEM,) * 4 + (SMEM,) * 2,
        scratch_shapes=[
            pltpu.VMEM((32, C), jnp.float32),
            pltpu.VMEM((C, C), jnp.bfloat16),
            pltpu.VMEM((C, C), jnp.bfloat16),
            pltpu.VMEM((8 + ONES, BLK), jnp.float32),
        ],
        compiler_params=PARAMS,
        cost_estimate=pl.CostEstimate(flops=n * 10**9, bytes_accessed=n * 10**6, transcendentals=0),
        name="windows_near",
    )(inner_a, inner_b, outer_a, outer_b, gain, w_qkv)


def tops(scores, bounded):
    if bounded:
        return scores
    top = jnp.maximum(jnp.max(scores[0], axis=0, keepdims=True), jnp.max(scores[1], axis=0, keepdims=True))
    return [score - top for score in scores]


def mix(scores, values, slots, queries_n):
    parts = [dot_nn(value, jnp.exp(score).astype(jnp.bfloat16)) for score, value in zip(scores, values)]
    summed = parts[0] + parts[1]
    n = summed.shape[0] - ONES
    total = summed[n : n + 1, :] + jnp.where(slots < queries_n, 0.0, 1.0)
    return summed[:n, :] * (1.0 / total)


def far_kernel(first, n, flags, counts, peaks, far_a, far_b, gain, w_qkv, w_out, k_near, vt_near, qt, spread, *refs):
    if len(refs) > 9:
        state, inner, result, ranks, k_far, vt_far, wvt, woutt, norms, mixes, count_far, out, sums, sems = refs
    else:
        out, ranks, k_far, vt_far, wvt, woutt, norms, mixes, count_far = refs
    far_refs = (far_a, far_b)

    def tokens_at(w, s):
        i = jnp.where(flags[1] == 1, n - 1 - w, w) if s == 1 else w
        return far_refs[s][pl.ds(2 * i, 2)].reshape(HALF, C)

    rank = ocean_ranks([tokens_at(i // 2, i % 2) for i in range(2 * n)], 16)
    ranks[...] = rank
    for i in range(2 * n):
        found = jnp.max(rank[i : i + 1, :]).astype(jnp.int32)
        count_far[i] = jnp.where(flags[0] == 1, 0, found) if i % 2 else found
    eye = one(iota((C, C), 0) == iota((C, C), 1))
    wvt[...] = dot_nt(eye, w_qkv[:, 2 * C :]).astype(jnp.bfloat16)
    woutt[...] = dot_nt(eye, w_out[...]).astype(jnp.bfloat16)
    norms[...] = jnp.zeros_like(norms)

    def prepare(size, items, span):
        sums = one(iota((C, BLK), 0) // HEAD == iota((C, BLK), 1))
        count = [count_far[2 * w + s] for w, s in items]
        normed = [
            packed_norm(tokens_at(w, s), ranks[pl.ds(2 * w + s, 1), :], c, size, gain[...]) for (w, s), c in zip(items, count)
        ]
        keys = [dot_nn(x, w_qkv[:, C : 2 * C]).astype(jnp.bfloat16) for x in normed]
        values = [dot_nt(wvt[...], valid_rows(x, c)).astype(jnp.bfloat16) for x, c in zip(normed, count)]
        for (w, s), c, key, value in zip(items, count, keys, values):
            k_far[2 * w + s, :size, :] = key
            vt_far[2 * w + s, :C, :size] = value
            vt_far[2 * w + s, C:, :size] = valid_ones(c, size)
            if size < HALF:
                fill(k_far, vt_far, 2 * w + s, key, size)
            norms[0:1, :] = jnp.maximum(norms[0:1, :], head_norms(key, sums))

    for_halves(((0, n),), count_far, prepare)
    peak = jnp.maximum(jnp.max(norms[0:1, :]), peaks[0]) * peaks[1]
    largest_weight = jnp.max(jnp.abs(w_qkv[:, 2 * C :].astype(jnp.float32)))
    asked_from = counts.shape[0] // 2
    safe = (peak <= SAFE_SQ) & (largest_weight <= SAFE_WEIGHT)

    lane = iota((1, C), 1)

    def attend(w, halves, size, bounded, fused):
        at = {k: 2 * w + s for k, s in halves.items()}
        near_at = {k: 2 * first + i for k, i in at.items()}
        asked = {k: counts[asked_from + i] for k, i in near_at.items()}
        keys = {s: [k_near[near_at[s], :size, :], k_far[at[s], :size, :]] for s in halves}
        if not bounded:
            for s in halves:
                near, far = [key.astype(jnp.float32) for key in keys[s]]
                far = jnp.where(count_far[at[s]] > 0, far, jnp.broadcast_to(near[0:1], far.shape))
                keys[s][1] = far.astype(jnp.bfloat16)

        def values(s, rows):
            return [
                jnp.concatenate([ref[i, rows, :size], ref[i, C : C + ONES, :size]], axis=0)
                for ref, i in ((vt_near, near_at[s]), (vt_far, at[s]))
            ]

        def base_scores(t, s):
            g = t // 2
            none = jnp.zeros((HEAD, BLK), jnp.bfloat16)
            rows = []
            for h in range(4 * g, 4 * g + 4):
                mine = qt[near_at[s], HEAD * h : HEAD * h + HEAD, :BLK] if h // 2 == t else none
                rows.append(jnp.concatenate([mine, none] if h % 2 == 0 else [none, mine], axis=1))
            stacked = jnp.concatenate(rows, axis=0)
            return [dot_nn(key[:, BLK * g : BLK * g + BLK], stacked) for key in keys[s]]

        sub, lan = iota((C, C), 0), iota((C, C), 1)
        block = sub // HEAD == lan // QB

        def rest_stacked(start, s):
            repeat = one(sub[:BLK] + BLK == start + lan[:BLK] % QB)
            return jnp.where(block, dot_nn(qt[near_at[s], :, BLK:], repeat), 0.0).astype(jnp.bfloat16)

        def rest_mixed(start, s, scores):
            mixed = mix(tops(scores, bounded), values(s, slice(0, C)), start + lane % QB, asked[s])
            mixed = jnp.where(block, mixed, 0.0).astype(jnp.bfloat16)
            return dot_nn(mixed, one(sub[:, :BLK] % QB + start == lan[:, :BLK] + BLK))

        def rolled(s):
            none = jnp.zeros((HEAD, BLK), jnp.float32)
            rows = []
            for h in range(HEADS):
                x = qt[near_at[s], HEAD * h : HEAD * h + HEAD, BLK:].astype(jnp.float32)
                x = jnp.where(iota((HEAD, BLK), 1) < QB, x, 0.0)
                x = pltpu.roll(x, QB * (h % 4), 1) if h % 4 else x
                rows.append(jnp.concatenate([x, none] if h < 4 else [none, x], axis=1))
            return jnp.concatenate(rows, axis=0).astype(jnp.bfloat16)

        def unroll(s, mixed):
            for h in range(HEADS):
                piece = mixed[HEAD * h : HEAD * h + HEAD, BLK * (h // 4) : BLK * (h // 4) + BLK]
                piece = pltpu.roll(piece, BLK - QB * (h % 4), 1) if h % 4 else piece
                piece = jnp.where(iota((HEAD, BLK), 1) < QB, piece, 0.0)
                mixes[at[s], HEAD * h : HEAD * h + HEAD, BLK:] = piece.astype(jnp.bfloat16)

        tiles = [(t, s) for t in range(4) for s in halves]
        if fused:
            stacked = {s: rolled(s) for s in halves}
            tiles = tiles[:2] + [(4, s) for s in halves] + tiles[2:]

        def tile_scores(t, s):
            return [dot_nn(key, stacked[s]) for key in keys[s]] if t == 4 else base_scores(t, s)

        ahead = tile_scores(*tiles[0])
        for i, (t, s) in enumerate(tiles):
            now = ahead
            if i + 1 < len(tiles):
                ahead = tile_scores(*tiles[i + 1])
            if t == 4:
                unroll(s, mix(tops(now, bounded), values(s, slice(0, C)), BLK + lane % QB, asked[s]))
                continue
            mixed = mix(tops(now, bounded), values(s, slice(64 * t, 64 * t + 64)), lane % BLK, asked[s])
            mixes[at[s], 64 * t : 64 * t + HEAD, :BLK] = mixed[:HEAD, :BLK].astype(jnp.bfloat16)
            mixes[at[s], 64 * t + HEAD : 64 * t + 64, :BLK] = mixed[HEAD:, BLK:].astype(jnp.bfloat16)
        if fused:
            return
        for s in halves:
            mixes[at[s], :, BLK:] = jnp.zeros((C, BLK), jnp.bfloat16)
        if bounded:
            return

        most = functools.reduce(jnp.maximum, asked.values())

        def more(b, carry):
            start = b * QB
            stacked = [rest_stacked(start, s) for s in halves]
            scores = [[dot_nn(key, x) for key in keys[s]] for s, x in zip(halves, stacked)]
            placed = [rest_mixed(start, s, score) for s, score in zip(halves, scores)]
            for s, x in zip(halves, placed):
                mixes[at[s], :, BLK:] = (mixes[at[s], :, BLK:].astype(jnp.float32) + x).astype(jnp.bfloat16)
            return carry

        lax.fori_loop(BLK // QB, (most + QB - 1) // QB, more, 0)

    def window(w, carry):
        at = 2 * first + 2 * w
        largest = jnp.maximum(jnp.maximum(counts[at], counts[at + 1]), jnp.maximum(count_far[2 * w], count_far[2 * w + 1]))
        most = jnp.maximum(counts[asked_from + at], counts[asked_from + at + 1])
        active = most > 0
        easy = safe & (largest <= SIZES[-1]) & (most <= BLK + QB)

        @pl.when(jnp.logical_not(active))
        def _():
            for s in range(2):
                mixes[2 * w + s] = jnp.zeros_like(mixes[2 * w + s])

        under = -1
        for size in SIZES:
            fits = active & easy & (largest > under) & (largest <= size)
            pl.when(fits & (most <= BLK))(functools.partial(attend, w, {0: 0, 1: 1}, size, True, False))
            pl.when(fits & (most > BLK))(functools.partial(attend, w, {0: 0, 1: 1}, size, True, True))
            under = size

        @pl.when(active & jnp.logical_not(easy))
        def _():
            def general(s, carry):
                attend(w, {0: s}, HALF, False, False)
                return carry

            lax.fori_loop(0, 2, general, 0)

        return carry

    lax.fori_loop(0, n, window, 0)

    for i in range(0, 2 * n, GROUP):
        items = [(j // 2, j % 2) for j in range(i, min(i + GROUP, 2 * n))]
        delta_t = [dot_nn(woutt[...], mixes[2 * w + s]).astype(jnp.bfloat16) for w, s in items]
        delta = [dot_nt(spread[2 * first + 2 * w + s], x) for (w, s), x in zip(items, delta_t)]
        for (w, s), x in zip(items, delta):
            if s == 1:
                x = jnp.where(flags[0] == 1, 0.0, x)
            out[w, s] = x.astype(jnp.bfloat16).reshape(2, BLK, C)

    if len(refs) > 9:
        finish(flags, state, inner, out, sums, result, sems)


def far_half(flags, near, far_a, far_b, gain, w_qkv, w_out, state=None, inner=None):
    k_near, vt_near, qt, spread, counts, peaks = near
    n = far_a.shape[0] // 2
    last = state is not None
    first = counts.shape[0] // 4 - n if last else 0
    deltas = (n, 2, 2, BLK, C)
    scratch = [
        pltpu.VMEM((16, C), jnp.float32),
        pltpu.VMEM((2 * n, HALF, C), jnp.bfloat16),
        pltpu.VMEM((2 * n, C + ONES, HALF), jnp.bfloat16),
        pltpu.VMEM((C, C), jnp.bfloat16),
        pltpu.VMEM((C, C), jnp.bfloat16),
        pltpu.VMEM((8, BLK), jnp.float32),
        pltpu.VMEM((2 * n, C, HALF), jnp.bfloat16),
        pltpu.SMEM((2 * n,), jnp.int32),
    ]
    if last:
        scratch += [pltpu.VMEM(deltas, jnp.bfloat16), pltpu.VMEM(state.shape, state.dtype), pltpu.SemaphoreType.DMA((8,))]
    return pl.pallas_call(
        functools.partial(far_kernel, first, n),
        out_shape=jax.ShapeDtypeStruct(state.shape if last else deltas, jnp.bfloat16),
        in_specs=[SMEM] * 3 + [VMEM] * (11 if last else 9),
        out_specs=ANY if last else VMEM,
        scratch_shapes=scratch,
        compiler_params=PARAMS,
        cost_estimate=pl.CostEstimate(flops=n * 10**9, bytes_accessed=n * 10**6, transcendentals=0),
        name="windows_edge" if last else "windows_inner",
    )(flags, counts, peaks, far_a, far_b, gain, w_qkv, w_out, k_near, vt_near, qt, spread, *((state, inner) if last else ()))


def permute(x, pairs):
    return lax.ppermute(x, ("lon", "lat"), pairs)


def shards(state, ocean_mask, norm_gain, w_qkv, w_out):
    lon_n, lat_n = lax.axis_size("lon"), lax.axis_size("lat")
    lat = lax.axis_index("lat")
    at = lambda i, j: i * lat_n + j
    every = [(i, j) for i in range(lon_n) for j in range(lat_n)]
    go_a = [(at(i, j), at(i, j - 1 if j % 2 else j + 1)) for i, j in every]
    go_b = [(at(i, j), at(i, j + 1 if j % 2 else j - 1)) for i, j in every if 0 < j < lat_n - 1]
    go_b += [(at(i, lat_n - 1), at(lon_n - 1 - i, lat_n - 1)) for i in range(lon_n)]
    go_east = [(at(i, j), at((i + 1) % lon_n, j)) for i, j in every]
    go_west = [(at(i, j), at((i - 1) % lon_n, j)) for i, j in every]

    flags = jnp.stack([lat == 0, lat == lat_n - 1, lat % 2 == 1]).astype(jnp.int32)
    inner_a, inner_b, outer_a, outer_b, to_east, to_west = prep(flags, state, ocean_mask, RIM)
    west = permute(to_east, go_east)
    east = permute(to_west, go_west)
    far_a = permute(inner_a, go_a)
    far_b = permute(inner_b, go_b)
    rim = lambda x, s: jnp.concatenate([x[:1], west[s : s + 1], x[1:], east[s : s + 1]])
    outer_a, outer_b = rim(outer_a, 0), rim(outer_b, 1)
    rim_a = permute(outer_a, go_a)
    rim_b = permute(outer_b, go_b)

    gain = norm_gain[None, :]
    inner_a, inner_b, outer_a, outer_b = lax.optimization_barrier((inner_a, inner_b, outer_a, outer_b))
    near = near_half(inner_a, inner_b, outer_a, outer_b, gain, w_qkv)
    inner = far_half(flags, near, far_a, far_b, gain, w_qkv, w_out)
    return far_half(flags, near, rim_a, rim_b, gain, w_qkv, w_out, state, inner)


def solution(mesh):
    in_specs = (P(None, "lat", "lon", None), P(None, "lat", "lon"), P(), P(), P())
    out_specs = P(None, "lat", "lon", None)
    return jax.shard_map(shards, mesh=mesh, in_specs=in_specs, out_specs=out_specs, check_vma=False)
```

```python
import functools

import jax
import jax.numpy as jnp
from jax import lax
from jax.experimental import pallas as pl
from jax.experimental.pallas import tpu as pltpu
from jax.sharding import PartitionSpec as P

C = 256
HEADS = 8
HEAD = C // HEADS
W = 16
SHIFT = 8
LEV = 2
HALF = W * W * LEV // 2
BLK = HALF // 2
QB = 32
ONES = 16
SIZES = (144, 176)
GROUP = 10
RIM = 3
LAND = 1024.0
SAFE_SQ = 60.0**2
SAFE_WEIGHT = 1e6

VMEM = pl.BlockSpec(memory_space=pltpu.VMEM)
SMEM = pl.BlockSpec(memory_space=pltpu.SMEM)
ANY = pl.BlockSpec(memory_space=pl.ANY)
PARAMS = pltpu.CompilerParams(vmem_limit_bytes=36 * 1024 * 1024)


def dot_nt(a, b):
    return lax.dot_general(a, b, (((1,), (1,)), ((), ())), preferred_element_type=jnp.float32)


def dot_nn(a, b):
    return jnp.dot(a, b, preferred_element_type=jnp.float32)


def iota(shape, axis):
    return lax.broadcasted_iota(jnp.int32, shape, axis)


def one(condition):
    return jnp.where(condition, 1.0, 0.0).astype(jnp.bfloat16)


def ocean_ranks(halves, rows_n):
    channel, row = iota((rows_n, C), 1), iota((rows_n, C), 0)
    marks = None
    for i, half in enumerate(halves):
        part = dot_nt(one((channel == 0) & (row == i)), half)
        marks = part if marks is None else marks + part
    ocean = jnp.where(marks < LAND / 2, 1.0, 0.0)
    return dot_nn(ocean.astype(jnp.bfloat16), one(iota((C, C), 0) <= iota((C, C), 1))) * ocean


def packed_norm(tokens, ranks, count, size, gain):
    wanted = jnp.minimum(iota((size, 1), 0) + 1, count).astype(jnp.float32)
    packed = dot_nn(one(ranks == wanted), tokens)
    average = jnp.mean(packed, axis=1, keepdims=True)
    centred = packed - average
    spread_sq = jnp.mean(centred * centred, axis=1, keepdims=True)
    return (centred * lax.rsqrt(spread_sq + 1e-05) * gain).astype(jnp.bfloat16)


def valid_rows(x, count):
    return jnp.where(iota((x.shape[0], 1), 0) < count, x.astype(jnp.float32), 0.0).astype(jnp.bfloat16)


def valid_ones(count, size):
    return one(jnp.broadcast_to(iota((1, size), 1) < count, (ONES, size)))


def head_norms(keys, sums):
    return jnp.max(dot_nn((keys * keys).astype(jnp.bfloat16), sums), axis=0, keepdims=True)


def fill(keys, values, i, key, size):
    keys[i, size:, :] = jnp.broadcast_to(key[0:1].astype(jnp.float32), (HALF - size, C)).astype(jnp.bfloat16)
    values[i, :, size:] = jnp.zeros((C + ONES, HALF - size), jnp.bfloat16)


def prep_kernel(flags, state, mask, inner_a, inner_b, outer_a, outer_b, to_east, to_west):
    blocks = state.shape[2] // SHIFT
    cols = blocks * SHIFT
    rim = outer_a.shape[0] // 2
    eye = one(iota((cols, cols), 0) == iota((cols, cols), 1))
    by_column = [dot_nt(eye, mask[level]).astype(jnp.bfloat16) for level in range(LEV)]
    for s, inner, outer in ((0, inner_a, outer_a), (1, inner_b, outer_b)):
        first = jnp.where(flags[2] == s, SHIFT, 0)
        for level in range(LEV):
            for p in range(SHIFT // 2):
                pair = []
                for row in (2 * p, 2 * p + 1):
                    chosen = one(iota((2 * SHIFT, BLK), 0) == first + row)
                    ocean = dot_nn(by_column[level], chosen)
                    ocean = jnp.concatenate([ocean, ocean], axis=1)
                    values = state[level, first + row].astype(jnp.float32)
                    pair.append(jnp.where(ocean > 0.5, values, LAND).reshape(blocks, SHIFT, C))
                both = jnp.concatenate(pair, axis=1).astype(jnp.bfloat16)
                at = pl.ds((BLK // 2) * level + 2 * SHIFT * p, 2 * SHIFT)
                inner[:, at, :] = both[rim : blocks - rim]
                outer[:rim, at, :] = both[:rim]
                outer[rim:, at, :] = both[blocks - rim :]
                to_east[s, at, :] = both[blocks - 1]
                to_west[s, at, :] = both[0]


def prep(flags, state, mask, rim):
    blocks = state.shape[2] // SHIFT
    shape = lambda n: jax.ShapeDtypeStruct((n, BLK, C), jnp.bfloat16)
    return pl.pallas_call(
        prep_kernel,
        out_shape=(shape(blocks - 2 * rim),) * 2 + (shape(2 * rim),) * 2 + (shape(2),) * 2,
        in_specs=[SMEM, VMEM, VMEM],
        out_specs=(VMEM,) * 6,
        compiler_params=PARAMS,
        name="windows_prep",
    )(flags, state, mask.astype(jnp.bfloat16))


def finish(flags, state, inner, outer, sums, out, sems):
    blocks = state.shape[2] // SHIFT
    rim = (blocks - 2 * inner.shape[0]) // 2
    half = SHIFT // 2
    copies = []
    for level in range(LEV):
        for quarter in range(state.shape[1] // half):
            s = flags[2] if quarter // 2 == 1 else 1 - flags[2]
            for p in range(half // 2):
                at = pl.ds(level * (BLK // 2) + SHIFT * (half * (quarter % 2) + 2 * p), 2 * SHIFT)
                deltas = []
                for b in range(blocks):
                    if b < rim:
                        delta = outer[(b + 1) // 2, s, 0 if b == 0 else 1 - b % 2, at, :]
                    elif b < blocks - rim:
                        delta = inner[(b - rim) // 2, s, (b - rim) % 2, at, :]
                    else:
                        k = b - (blocks - rim)
                        delta = outer[(rim + 1) // 2 + k // 2, s, k % 2, at, :]
                    deltas.append(delta.astype(jnp.float32))
                for i in range(2):
                    added = jnp.concatenate([d[SHIFT * i : SHIFT * i + SHIFT] for d in deltas], axis=0)
                    row = half * quarter + 2 * p + i
                    sums[level, row] = (state[level, row].astype(jnp.float32) + added).astype(jnp.bfloat16)
            rows = pl.ds(half * quarter, half)
            copies.append(pltpu.make_async_copy(sums.at[level, rows], out.at[level, rows], sems.at[len(copies)]))
            copies[-1].start()
    for copy in copies:
        copy.wait()


def for_halves(spans, counts, work):
    largest = functools.reduce(jnp.maximum, [counts[i] for i in range(2 * spans[0][0], 2 * spans[-1][1])])
    size = SIZES[-1]

    @pl.when(largest <= size)
    def _():
        for i, (start, end) in enumerate(spans):
            items = [(w, s) for w in range(start, end) for s in range(2)]
            for at in range(0, len(items), GROUP):
                work(size, items[at : at + GROUP], i)

    @pl.when(largest > size)
    def _():
        for i, (start, end) in enumerate(spans):

            def step(w, carry, i=i):
                work(HALF, [(w, 0), (w, 1)], i)
                return carry

            lax.fori_loop(start, end, step, 0)


def near_kernel(spans, inner_a, inner_b, outer_a, outer_b, gain, w_qkv, k_out, vt_out, qt_out, spread_out, counts, peaks, ranks, wqt, wvt, norms):
    parts = ((inner_a, inner_b), (outer_a, outer_b))
    n = spans[-1][1]

    def tokens_at(w, s, span):
        return parts[span][s][pl.ds(2 * (w - spans[span][0]), 2)].reshape(HALF, C)

    halves = [(w, s, i) for i, (start, end) in enumerate(spans) for w in range(start, end) for s in range(2)]
    rank = ocean_ranks([tokens_at(*half) for half in halves], 32)
    ranks[...] = rank
    for i in range(2 * n):
        counts[i] = jnp.max(rank[i : i + 1, :]).astype(jnp.int32)
        is_edge = i // 2 in (spans[1][0], n - 1)
        counts[2 * n + i] = jnp.max(rank[i : i + 1, :BLK]).astype(jnp.int32) if is_edge else counts[i]

    eye = one(iota((C, C), 0) == iota((C, C), 1))
    wqt[...] = dot_nt(eye, w_qkv[:, :C]).astype(jnp.bfloat16)
    wvt[...] = dot_nt(eye, w_qkv[:, 2 * C :]).astype(jnp.bfloat16)
    norms[...] = jnp.zeros_like(norms)
    by_column = dot_nt(eye, rank.astype(jnp.bfloat16)).astype(jnp.bfloat16)
    for i in range(2 * n):
        col_rank = dot_nn(by_column, one(iota((32, BLK), 0) == i))
        for at in (0, BLK):
            number = (iota((HALF, BLK), 1) + (at + 1)).astype(jnp.float32)
            spread_out[i, :, at : at + BLK] = one(col_rank == number)

    def window(size, items, span):
        sums = one(iota((C, BLK), 0) // HEAD == iota((C, BLK), 1))
        sums_t = one(iota((ONES, C), 1) // HEAD == iota((ONES, C), 0))
        count = [counts[2 * w + s] for w, s in items]
        normed = [
            packed_norm(tokens_at(w, s, span), ranks[pl.ds(2 * w + s, 1), :], c, size, gain[...]) for (w, s), c in zip(items, count)
        ]
        keys = [dot_nn(x, w_qkv[:, C : 2 * C]).astype(jnp.bfloat16) for x in normed]
        queries = [(dot_nt(wqt[...], x) * (1.0 / HEAD**0.5)).astype(jnp.bfloat16) for x in normed]
        values = [dot_nt(wvt[...], valid_rows(x, c)).astype(jnp.bfloat16) for x, c in zip(normed, count)]
        for (w, s), c, key, query, value in zip(items, count, keys, queries, values):
            k_out[2 * w + s, :size, :] = key
            qt_out[2 * w + s, :, :size] = query
            vt_out[2 * w + s, :C, :size] = value
            vt_out[2 * w + s, C:, :size] = valid_ones(c, size)
            if size < HALF:
                qt_out[2 * w + s, :, size:] = jnp.zeros((C, HALF - size), jnp.bfloat16)
                fill(k_out, vt_out, 2 * w + s, key, size)
            norms[0:1, :] = jnp.maximum(norms[0:1, :], head_norms(key, sums))
            by_head = dot_nn(sums_t, query * query)
            norms[8:, :] = jnp.maximum(norms[8:, :], jnp.max(by_head, axis=1, keepdims=True))

    for_halves(spans, counts, window)
    peaks[0] = jnp.max(norms[0:1, :])
    peaks[1] = jnp.max(norms[8:, :])


def near_half(inner_a, inner_b, outer_a, outer_b, gain, w_qkv):
    middle = inner_a.shape[0] // 2
    n = middle + outer_a.shape[0] // 2
    bf = lambda *shape: jax.ShapeDtypeStruct(shape, jnp.bfloat16)
    return pl.pallas_call(
        functools.partial(near_kernel, ((0, middle), (middle, n))),
        out_shape=(
            bf(2 * n, HALF, C),
            bf(2 * n, C + ONES, HALF),
            bf(2 * n, C, HALF),
            bf(2 * n, HALF, HALF),
            jax.ShapeDtypeStruct((4 * n,), jnp.int32),
            jax.ShapeDtypeStruct((2,), jnp.float32),
        ),
        in_specs=[VMEM] * 6,
        out_specs=(VMEM,) * 4 + (SMEM,) * 2,
        scratch_shapes=[
            pltpu.VMEM((32, C), jnp.float32),
            pltpu.VMEM((C, C), jnp.bfloat16),
            pltpu.VMEM((C, C), jnp.bfloat16),
            pltpu.VMEM((8 + ONES, BLK), jnp.float32),
        ],
        compiler_params=PARAMS,
        cost_estimate=pl.CostEstimate(flops=n * 10**9, bytes_accessed=n * 10**6, transcendentals=0),
        name="windows_near",
    )(inner_a, inner_b, outer_a, outer_b, gain, w_qkv)


def tops(scores, bounded):
    if bounded:
        return scores
    top = jnp.maximum(jnp.max(scores[0], axis=0, keepdims=True), jnp.max(scores[1], axis=0, keepdims=True))
    return [score - top for score in scores]


def mix(scores, values, slots, queries_n):
    parts = [dot_nn(value, jnp.exp(score).astype(jnp.bfloat16)) for score, value in zip(scores, values)]
    summed = parts[0] + parts[1]
    n = summed.shape[0] - ONES
    total = summed[n : n + 1, :] + jnp.where(slots < queries_n, 0.0, 1.0)
    return summed[:n, :] * (1.0 / total)


def far_kernel(first, n, flags, counts, peaks, far_a, far_b, gain, w_qkv, w_out, k_near, vt_near, qt, spread, *refs):
    if len(refs) > 9:
        state, inner, result, ranks, k_far, vt_far, wvt, woutt, norms, mixes, count_far, out, sums, sems = refs
    else:
        out, ranks, k_far, vt_far, wvt, woutt, norms, mixes, count_far = refs
    far_refs = (far_a, far_b)

    def tokens_at(w, s):
        i = jnp.where(flags[1] == 1, n - 1 - w, w) if s == 1 else w
        return far_refs[s][pl.ds(2 * i, 2)].reshape(HALF, C)

    rank = ocean_ranks([tokens_at(i // 2, i % 2) for i in range(2 * n)], 16)
    ranks[...] = rank
    for i in range(2 * n):
        found = jnp.max(rank[i : i + 1, :]).astype(jnp.int32)
        count_far[i] = jnp.where(flags[0] == 1, 0, found) if i % 2 else found
    eye = one(iota((C, C), 0) == iota((C, C), 1))
    wvt[...] = dot_nt(eye, w_qkv[:, 2 * C :]).astype(jnp.bfloat16)
    woutt[...] = dot_nt(eye, w_out[...]).astype(jnp.bfloat16)
    norms[...] = jnp.zeros_like(norms)

    def prepare(size, items, span):
        sums = one(iota((C, BLK), 0) // HEAD == iota((C, BLK), 1))
        count = [count_far[2 * w + s] for w, s in items]
        normed = [
            packed_norm(tokens_at(w, s), ranks[pl.ds(2 * w + s, 1), :], c, size, gain[...]) for (w, s), c in zip(items, count)
        ]
        keys = [dot_nn(x, w_qkv[:, C : 2 * C]).astype(jnp.bfloat16) for x in normed]
        values = [dot_nt(wvt[...], valid_rows(x, c)).astype(jnp.bfloat16) for x, c in zip(normed, count)]
        for (w, s), c, key, value in zip(items, count, keys, values):
            k_far[2 * w + s, :size, :] = key
            vt_far[2 * w + s, :C, :size] = value
            vt_far[2 * w + s, C:, :size] = valid_ones(c, size)
            if size < HALF:
                fill(k_far, vt_far, 2 * w + s, key, size)
            norms[0:1, :] = jnp.maximum(norms[0:1, :], head_norms(key, sums))

    for_halves(((0, n),), count_far, prepare)
    peak = jnp.maximum(jnp.max(norms[0:1, :]), peaks[0]) * peaks[1]
    largest_weight = jnp.max(jnp.abs(w_qkv[:, 2 * C :].astype(jnp.float32)))
    asked_from = counts.shape[0] // 2
    safe = (peak <= SAFE_SQ) & (largest_weight <= SAFE_WEIGHT)

    lane = iota((1, C), 1)

    def attend(w, halves, size, bounded, fused):
        at = {k: 2 * w + s for k, s in halves.items()}
        near_at = {k: 2 * first + i for k, i in at.items()}
        asked = {k: counts[asked_from + i] for k, i in near_at.items()}
        keys = {s: [k_near[near_at[s], :size, :], k_far[at[s], :size, :]] for s in halves}
        if not bounded:
            for s in halves:
                near, far = [key.astype(jnp.float32) for key in keys[s]]
                far = jnp.where(count_far[at[s]] > 0, far, jnp.broadcast_to(near[0:1], far.shape))
                keys[s][1] = far.astype(jnp.bfloat16)

        def values(s, rows):
            return [
                jnp.concatenate([ref[i, rows, :size], ref[i, C : C + ONES, :size]], axis=0)
                for ref, i in ((vt_near, near_at[s]), (vt_far, at[s]))
            ]

        def base_scores(t, s):
            g = t // 2
            none = jnp.zeros((HEAD, BLK), jnp.bfloat16)
            rows = []
            for h in range(4 * g, 4 * g + 4):
                mine = qt[near_at[s], HEAD * h : HEAD * h + HEAD, :BLK] if h // 2 == t else none
                rows.append(jnp.concatenate([mine, none] if h % 2 == 0 else [none, mine], axis=1))
            stacked = jnp.concatenate(rows, axis=0)
            return [dot_nn(key[:, BLK * g : BLK * g + BLK], stacked) for key in keys[s]]

        sub, lan = iota((C, C), 0), iota((C, C), 1)
        block = sub // HEAD == lan // QB

        def rest_stacked(start, s):
            repeat = one(sub[:BLK] + BLK == start + lan[:BLK] % QB)
            return jnp.where(block, dot_nn(qt[near_at[s], :, BLK:], repeat), 0.0).astype(jnp.bfloat16)

        def rest_mixed(start, s, scores):
            mixed = mix(tops(scores, bounded), values(s, slice(0, C)), start + lane % QB, asked[s])
            mixed = jnp.where(block, mixed, 0.0).astype(jnp.bfloat16)
            return dot_nn(mixed, one(sub[:, :BLK] % QB + start == lan[:, :BLK] + BLK))

        def rolled(s):
            none = jnp.zeros((HEAD, BLK), jnp.float32)
            rows = []
            for h in range(HEADS):
                x = qt[near_at[s], HEAD * h : HEAD * h + HEAD, BLK:].astype(jnp.float32)
                x = jnp.where(iota((HEAD, BLK), 1) < QB, x, 0.0)
                x = pltpu.roll(x, QB * (h % 4), 1) if h % 4 else x
                rows.append(jnp.concatenate([x, none] if h < 4 else [none, x], axis=1))
            return jnp.concatenate(rows, axis=0).astype(jnp.bfloat16)

        def unroll(s, mixed):
            for h in range(HEADS):
                piece = mixed[HEAD * h : HEAD * h + HEAD, BLK * (h // 4) : BLK * (h // 4) + BLK]
                piece = pltpu.roll(piece, BLK - QB * (h % 4), 1) if h % 4 else piece
                piece = jnp.where(iota((HEAD, BLK), 1) < QB, piece, 0.0)
                mixes[at[s], HEAD * h : HEAD * h + HEAD, BLK:] = piece.astype(jnp.bfloat16)

        tiles = [(t, s) for t in range(4) for s in halves]
        if fused:
            stacked = {s: rolled(s) for s in halves}
            tiles = tiles[:2] + [(4, s) for s in halves] + tiles[2:]

        def tile_scores(t, s):
            return [dot_nn(key, stacked[s]) for key in keys[s]] if t == 4 else base_scores(t, s)

        ahead = [tile_scores(*tile) for tile in tiles[:3]]
        for i, (t, s) in enumerate(tiles):
            now = ahead.pop(0)
            if i + 3 < len(tiles):
                ahead.append(tile_scores(*tiles[i + 3]))
            if t == 4:
                unroll(s, mix(tops(now, bounded), values(s, slice(0, C)), BLK + lane % QB, asked[s]))
                continue
            mixed = mix(tops(now, bounded), values(s, slice(64 * t, 64 * t + 64)), lane % BLK, asked[s])
            mixes[at[s], 64 * t : 64 * t + HEAD, :BLK] = mixed[:HEAD, :BLK].astype(jnp.bfloat16)
            mixes[at[s], 64 * t + HEAD : 64 * t + 64, :BLK] = mixed[HEAD:, BLK:].astype(jnp.bfloat16)
        if fused:
            return
        for s in halves:
            mixes[at[s], :, BLK:] = jnp.zeros((C, BLK), jnp.bfloat16)
        if bounded:
            return

        most = functools.reduce(jnp.maximum, asked.values())

        def more(b, carry):
            start = b * QB
            stacked = [rest_stacked(start, s) for s in halves]
            scores = [[dot_nn(key, x) for key in keys[s]] for s, x in zip(halves, stacked)]
            placed = [rest_mixed(start, s, score) for s, score in zip(halves, scores)]
            for s, x in zip(halves, placed):
                mixes[at[s], :, BLK:] = (mixes[at[s], :, BLK:].astype(jnp.float32) + x).astype(jnp.bfloat16)
            return carry

        lax.fori_loop(BLK // QB, (most + QB - 1) // QB, more, 0)

    def window(w, carry):
        at = 2 * first + 2 * w
        largest = jnp.maximum(jnp.maximum(counts[at], counts[at + 1]), jnp.maximum(count_far[2 * w], count_far[2 * w + 1]))
        most = jnp.maximum(counts[asked_from + at], counts[asked_from + at + 1])
        active = most > 0
        easy = safe & (largest <= SIZES[-1]) & (most <= BLK + QB)

        @pl.when(jnp.logical_not(active))
        def _():
            for s in range(2):
                mixes[2 * w + s] = jnp.zeros_like(mixes[2 * w + s])

        under = -1
        for size in SIZES:
            fits = active & easy & (largest > under) & (largest <= size)
            pl.when(fits & (most <= BLK))(functools.partial(attend, w, {0: 0, 1: 1}, size, True, False))
            pl.when(fits & (most > BLK))(functools.partial(attend, w, {0: 0, 1: 1}, size, True, True))
            under = size

        @pl.when(active & jnp.logical_not(easy))
        def _():
            def general(s, carry):
                attend(w, {0: s}, HALF, False, False)
                return carry

            lax.fori_loop(0, 2, general, 0)

        return carry

    lax.fori_loop(0, n, window, 0)

    for i in range(0, 2 * n, GROUP):
        items = [(j // 2, j % 2) for j in range(i, min(i + GROUP, 2 * n))]
        delta_t = [dot_nn(woutt[...], mixes[2 * w + s]).astype(jnp.bfloat16) for w, s in items]
        delta = [dot_nt(spread[2 * first + 2 * w + s], x) for (w, s), x in zip(items, delta_t)]
        for (w, s), x in zip(items, delta):
            if s == 1:
                x = jnp.where(flags[0] == 1, 0.0, x)
            out[w, s] = x.astype(jnp.bfloat16).reshape(2, BLK, C)

    if len(refs) > 9:
        finish(flags, state, inner, out, sums, result, sems)


def far_half(flags, near, far_a, far_b, gain, w_qkv, w_out, state=None, inner=None):
    k_near, vt_near, qt, spread, counts, peaks = near
    n = far_a.shape[0] // 2
    last = state is not None
    first = counts.shape[0] // 4 - n if last else 0
    deltas = (n, 2, 2, BLK, C)
    scratch = [
        pltpu.VMEM((16, C), jnp.float32),
        pltpu.VMEM((2 * n, HALF, C), jnp.bfloat16),
        pltpu.VMEM((2 * n, C + ONES, HALF), jnp.bfloat16),
        pltpu.VMEM((C, C), jnp.bfloat16),
        pltpu.VMEM((C, C), jnp.bfloat16),
        pltpu.VMEM((8, BLK), jnp.float32),
        pltpu.VMEM((2 * n, C, HALF), jnp.bfloat16),
        pltpu.SMEM((2 * n,), jnp.int32),
    ]
    if last:
        scratch += [pltpu.VMEM(deltas, jnp.bfloat16), pltpu.VMEM(state.shape, state.dtype), pltpu.SemaphoreType.DMA((8,))]
    return pl.pallas_call(
        functools.partial(far_kernel, first, n),
        out_shape=jax.ShapeDtypeStruct(state.shape if last else deltas, jnp.bfloat16),
        in_specs=[SMEM] * 3 + [VMEM] * (11 if last else 9),
        out_specs=ANY if last else VMEM,
        scratch_shapes=scratch,
        compiler_params=PARAMS,
        cost_estimate=pl.CostEstimate(flops=n * 10**9, bytes_accessed=n * 10**6, transcendentals=0),
        name="windows_edge" if last else "windows_inner",
    )(flags, counts, peaks, far_a, far_b, gain, w_qkv, w_out, k_near, vt_near, qt, spread, *((state, inner) if last else ()))


def permute(x, pairs):
    return lax.ppermute(x, ("lon", "lat"), pairs)


def shards(state, ocean_mask, norm_gain, w_qkv, w_out):
    lon_n, lat_n = lax.axis_size("lon"), lax.axis_size("lat")
    lat = lax.axis_index("lat")
    at = lambda i, j: i * lat_n + j
    every = [(i, j) for i in range(lon_n) for j in range(lat_n)]
    go_a = [(at(i, j), at(i, j - 1 if j % 2 else j + 1)) for i, j in every]
    go_b = [(at(i, j), at(i, j + 1 if j % 2 else j - 1)) for i, j in every if 0 < j < lat_n - 1]
    go_b += [(at(i, lat_n - 1), at(lon_n - 1 - i, lat_n - 1)) for i in range(lon_n)]
    go_east = [(at(i, j), at((i + 1) % lon_n, j)) for i, j in every]
    go_west = [(at(i, j), at((i - 1) % lon_n, j)) for i, j in every]

    flags = jnp.stack([lat == 0, lat == lat_n - 1, lat % 2 == 1]).astype(jnp.int32)
    inner_a, inner_b, outer_a, outer_b, to_east, to_west = prep(flags, state, ocean_mask, RIM)
    west = permute(to_east, go_east)
    east = permute(to_west, go_west)
    far_a = permute(inner_a, go_a)
    far_b = permute(inner_b, go_b)
    rim = lambda x, s: jnp.concatenate([x[:1], west[s : s + 1], x[1:], east[s : s + 1]])
    outer_a, outer_b = rim(outer_a, 0), rim(outer_b, 1)
    rim_a = permute(outer_a, go_a)
    rim_b = permute(outer_b, go_b)

    gain = norm_gain[None, :]
    inner_a, inner_b, outer_a, outer_b = lax.optimization_barrier((inner_a, inner_b, outer_a, outer_b))
    near = near_half(inner_a, inner_b, outer_a, outer_b, gain, w_qkv)
    inner = far_half(flags, near, far_a, far_b, gain, w_qkv, w_out)
    return far_half(flags, near, rim_a, rim_b, gain, w_qkv, w_out, state, inner)


def solution(mesh):
    in_specs = (P(None, "lat", "lon", None), P(None, "lat", "lon"), P(), P(), P())
    out_specs = P(None, "lat", "lon", None)
    return jax.shard_map(shards, mesh=mesh, in_specs=in_specs, out_specs=out_specs, check_vma=False)
```
